512 devices in a mesh: seg: 128 (over z, x, y_hi, core), head: 4 (over y_lo).
Axes of the slice: x: 4, y: 8 (y_hi: 2, y_lo: 4; y = y_hi * 4 + y_lo), z: 8, core: 2. Of those that a mesh axis runs over, the one named last changes fastest.
Arguments:
- layer_input: bfloat16 [1, 65536, 2048], P(None, 'seg', 'head'), may hold values from -160 to 160, as said below
- w_qkv: bfloat16 [2048, 3, 1024], P(None, None, 'head'), may hold values from -3 to 3
- comp_weight: bfloat16 [3, 2, 1024], P(None, None, 'head'), may hold values from -2.5 to 2.5
- w_out: bfloat16 [1024, 2048], P('seg', 'head'), may hold values from -1.5 to 1.5
Outputs:
- attn_out: bfloat16 [1, 65536, 2048], P(None, 'seg', 'head')
The draws below stay inside these ranges and needn't reach their ends.
Inputs may be any that keep to these rules, and one draw needn't show every extreme that they name: layer_input varies in scale from feature to feature and from token to token.
All inputs are finite; a program needn't handle non-finite values.
Results may differ from the reference program's by a relative error of at most 0.0089.
Values may be sent and summed in bfloat16 or wider, within the bound.
A program may use at most 64 MiB of HBM per device.

```python
import math
import jax
import jax.numpy as jnp
from jax import lax

D = 2048
HEADS = 8
DH = 128
SEG_LEN = 512
BOOKS = 1
HD = 1024
TOKENS = 65536
N_SEG = 128


def draw_layer_input(key, part):
    key_col, key_row, key_base = jax.random.split(key, 3)
    shape = (BOOKS, TOKENS, D)
    col_scale = jnp.exp(jax.random.uniform(key_col, (D,), jnp.float32, 0.0, math.log(10.0)))
    row_scale = jnp.exp(jax.random.uniform(key_row, (BOOKS, TOKENS, 1), jnp.float32, 0.0, math.log(4.0)))
    base = jax.random.truncated_normal(key_base, -4.0, 4.0, shape, jnp.float32)
    return jnp.clip(base * col_scale * row_scale, -160.0, 160.0).astype(jnp.bfloat16)


def draw_w_qkv(key, part):
    key_base = jax.random.fold_in(key, 0)
    base = jax.random.truncated_normal(key_base, -4.0, 4.0, (D, 3, HD), jnp.float32) / math.sqrt(D)
    return jnp.clip(base, -3.0, 3.0).astype(jnp.bfloat16)


def shard_levels(stream_key, extent, pieces, least, top_value):
    gain = 1.0
    for dim, blocks in pieces:
        draws = jax.random.uniform(jax.random.fold_in(jax.random.fold_in(stream_key, 6), dim), (blocks,), jnp.float32, least / len(pieces), top_value / len(pieces))
        gain = gain * jnp.repeat(jnp.exp(draws), extent[dim] // blocks).reshape((-1,) + (1,) * (len(extent) - 1 - dim))
    return gain


def scatter_about(own_key, shape, deviation, limit, cuts=(), kind=jnp.bfloat16):
    values = jax.random.normal(own_key, shape, jnp.float32) * deviation
    if len(cuts) > 0:
        values = shard_levels(own_key, shape, cuts, -0.22, 0.18) * values
    return jnp.clip(values, min=-limit, max=limit).astype(kind)


def setup_inputs(seed: int = 0) -> dict:
    seeds = jax.random.split(jax.random.key(seed), 5)
    layer_input = draw_layer_input(jax.random.fold_in(seeds[4], 71), 0)
    w_qkv = draw_w_qkv(jax.random.fold_in(seeds[4], 71), 0)
    comp_weight = scatter_about(seeds[2], (3, 2, HD), 0.6, 2.5, ((2, 4),))
    w_out = scatter_about(seeds[3], (HD, D), (HD // 64) ** -0.5, 1.5, ((0, 128), (1, 4)))
    return dict(layer_input=layer_input, w_qkv=w_qkv, comp_weight=comp_weight, w_out=w_out)


def layer_norm(values):
    center_mean = lax.optimization_barrier(jnp.mean(values, axis=-1, keepdims=True))
    centered = values - center_mean
    variance = lax.optimization_barrier(jnp.mean(centered * centered, axis=-1, keepdims=True))
    return centered * lax.rsqrt(variance + 1e-05)

def compress(source, weight):
    grouped = source.astype(jnp.float32).reshape(2, SEG_LEN, 3, HD)
    return jnp.einsum('kltc,tkc->klc', grouped, weight.astype(jnp.float32)).astype(jnp.bfloat16)

def key_allowed(segment):
    query_pos = jnp.arange(SEG_LEN)[:, None]
    key_pos = jnp.arange(3 * SEG_LEN)[None, :]
    own_part = (key_pos >= 2 * SEG_LEN) & (key_pos - 2 * SEG_LEN <= query_pos)
    memory_part = (key_pos >= SEG_LEN) & (key_pos < 2 * SEG_LEN) & (segment >= 1)
    comp_part = (key_pos < SEG_LEN) & (segment >= 4)
    return own_part | memory_part | comp_part

def attend(queries, keyed, valued, segment):
    query_heads = queries.astype(jnp.float32).reshape(SEG_LEN, HEADS, DH)
    key_heads = keyed.astype(jnp.float32).reshape(3 * SEG_LEN, HEADS, DH)
    value_heads = valued.astype(jnp.float32).reshape(3 * SEG_LEN, HEADS, DH)
    scores = jnp.einsum('qhd,khd->hqk', query_heads, key_heads) / math.sqrt(DH)
    scores = jnp.where(key_allowed(segment)[None], scores, jnp.float32(-1e+30))
    highest = lax.optimization_barrier(jnp.max(scores, axis=-1, keepdims=True))
    exponent = jnp.exp(scores - highest)
    weights = (exponent / lax.optimization_barrier(jnp.sum(exponent, axis=-1, keepdims=True))).astype(jnp.bfloat16)
    mixed = jnp.einsum('hqk,khd->qhd', weights.astype(jnp.float32), value_heads)
    return mixed.astype(jnp.bfloat16).reshape(SEG_LEN, HD)

def reference(layer_input, w_qkv, comp_weight, w_out):

    def one_book(book_rows):
        normed = layer_norm(book_rows.astype(jnp.float32)).astype(jnp.bfloat16)
        projected = jnp.dot(normed, w_qkv.reshape(D, 3 * HD), preferred_element_type=jnp.float32)
        projected = projected.astype(jnp.bfloat16).reshape(TOKENS, 3, HD)
        queries = projected[:, 0]
        key_vals = jnp.moveaxis(projected[:, 1:3], 1, 0)
        padded = jnp.concatenate([jnp.zeros((2, 4 * SEG_LEN, HD), jnp.bfloat16), key_vals], axis=1)

        def one_segment(segment):
            offset = (segment * SEG_LEN).astype(jnp.int32)
            window = lax.dynamic_slice_in_dim(padded, offset, 5 * SEG_LEN, 1)
            compressed = compress(window[:, :3 * SEG_LEN], comp_weight)
            joined = jnp.concatenate([compressed, window[:, 3 * SEG_LEN:]], axis=1)
            seg_queries = lax.dynamic_slice_in_dim(queries, offset, SEG_LEN, 0)
            context = attend(seg_queries, joined[0], joined[1], segment)
            return jnp.dot(context, w_out, preferred_element_type=jnp.float32).astype(jnp.bfloat16)
        outputs = lax.map(one_segment, jnp.arange(N_SEG, dtype=jnp.int32))
        return outputs.reshape(TOKENS, D)
    return lax.map(one_book, layer_input)
```

```python
import functools
import math

import jax
import jax.numpy as jnp
from jax import lax
from jax.experimental import pallas as pl
from jax.experimental.pallas import tpu as pltpu
from jax.sharding import PartitionSpec as P

MESH = pl.DeviceIdType.MESH
F32, BF16 = jnp.float32, jnp.bfloat16
DH = 128
RING = 8
SEG = 512
FEAT = 512
CX = 8
RX = SEG // CX
CC = 8
RC = SEG // CC
SCALE = math.log2(math.e) / math.sqrt(DH)
NT = (((1,), (1,)), ((), ()))


def dot(a, b):
    return jnp.dot(a, b, preferred_element_type=F32)


def kernel(n_seg, x_hbm, w_hbm, cw_ref, o_hbm, xb, wb, kv, wide, comp, nb, qb, cb,
           lsem, xs, xr, ks, kr, cs, cr):
    seg, lo = lax.axis_index("seg"), lax.axis_index("head")
    core, hi, block = seg % 2, (seg // 2) % 2, seg // 4
    y = hi * 4 + lo
    n_block = n_seg // 4

    def on_ring(pos):
        return (block * 4 + (pos // 4) * 2 + core, pos % 4)

    up, down = on_ring((y + 1) % RING), on_ring((y + RING - 1) % RING)
    sibling = (block * 4 + hi * 2 + 1 - core, lo)
    after, before = (block + 1) % n_block, (block + n_block - 1) % n_block
    after_same = (after * 4 + hi * 2 + core, lo)
    after_cross = (after * 4 + hi * 2 + 1 - core, lo)
    before_same = (before * 4 + hi * 2 + core, lo)
    before_cross = (before * 4 + hi * 2 + 1 - core, lo)

    own = pltpu.make_async_copy(x_hbm, xb.at[y], lsem.at[0])
    own.start()
    columns = pl.ds(pl.multiple_of(hi * DH, DH), DH)
    loads = []
    for i in range(3):
        load = pltpu.make_async_copy(
            w_hbm.at[i, :, columns], wb.at[:, pl.ds(i * DH, DH)], lsem.at[1 + i]
        )
        load.start()
        loads.append(load)

    barrier = pltpu.get_barrier_semaphore()
    others = (up, down, sibling, after_same, after_cross, before_same, before_cross)
    for other in others:
        pl.semaphore_signal(barrier, inc=1, device_id=other, device_id_type=MESH)
    pl.semaphore_wait(barrier, len(others))
    own.wait()

    def ring_copy(view, ssem, rsem, way, dist, chunk, hop):
        step = dist - hop
        slot = (y + RING - step) % RING if way == 0 else (y + step) % RING
        ref = view(slot, way, dist, chunk, hop)
        return pltpu.make_async_remote_copy(
            src_ref=ref,
            dst_ref=ref,
            send_sem=ssem.at[way, dist - 1, chunk],
            recv_sem=rsem.at[way, dist - 1, chunk],
            device_id=up if way == 0 else down,
            device_id_type=MESH,
        )

    def x_view(slot, way, dist, chunk, hop):
        if dist < 4:
            return xb.at[slot, pl.ds(pl.multiple_of(chunk * RX, RX), RX)]
        half = RX // 2
        return xb.at[slot, pl.ds(pl.multiple_of(chunk * RX + way * half, half), half)]

    def c_view(slot, way, dist, chunk, hop):
        if dist < 4:
            return cb.at[slot, :, pl.ds(pl.multiple_of(chunk * RC, RC), RC)]
        half = RC // 2
        unit = 1 - slot // 4
        return cb.at[slot, unit, pl.ds(pl.multiple_of(chunk * RC + way * half, half), half)]

    x_copy = functools.partial(ring_copy, x_view, xs, xr)
    c_copy = functools.partial(ring_copy, c_view, cs, cr)

    def forward(copy, i, count):
        for dist in (1, 2, 3):
            @pl.when((i >= dist) & (i < count + dist))
            def _(dist=dist):
                for way in (0, 1):
                    copy(way, dist, i - dist, 0).wait_recv()
                    copy(way, dist + 1, i - dist, 1).start()

    def landed(copy, i, count):
        for way in (0, 1):
            copy(way, 4, i - 4, 0).wait_recv()

    def kv_copies(chunk):
        rows = pl.ds(pl.multiple_of(chunk * RX, RX), RX)
        first_core = core == 0
        plan = (
            (4, jnp.where(first_core, 3, 5), sibling),
            (jnp.where(first_core, 6, 4), jnp.where(first_core, 5, 1),
             (jnp.where(first_core, sibling[0], after_cross[0]), lo)),
            (4, 0, after_same),
            (6, 2, after_same),
            (6, jnp.where(first_core, 1, 3), after_cross),
        )
        return [
            pltpu.make_async_remote_copy(
                src_ref=kv.at[src, rows],
                dst_ref=kv.at[dst, rows],
                send_sem=ks.at[n, chunk],
                recv_sem=kr.at[dst, chunk],
                device_id=device,
                device_id_type=MESH,
            )
            for n, (src, dst, device) in enumerate(plan)
        ]

    def project(chunk):
        rows = pl.ds(pl.multiple_of(chunk * RX, RX), RX)
        for u in range(2):
            parts = [xb[4 * u + f, rows, :].astype(F32) for f in range(4)]
            total = parts[0] + parts[1] + parts[2] + parts[3]
            mean = jnp.sum(total, axis=-1, keepdims=True) / (4 * FEAT)
            parts = [p - mean for p in parts]
            square = sum(p * p for p in parts[1:]) + parts[0] * parts[0]
            var = jnp.sum(square, axis=-1, keepdims=True) / (4 * FEAT)
            rstd = lax.rsqrt(var + 1e-05)
            for f in range(4):
                nb[u * RX:(u + 1) * RX, f * FEAT:(f + 1) * FEAT] = (parts[f] * rstd).astype(BF16)
        out = dot(nb[...], wb[...]).astype(BF16)
        for u in range(2):
            part = out[u * RX:(u + 1) * RX]
            qb[u, rows, :] = part[:, :DH]
            kv[4 + 2 * u, rows, :] = part[:, DH:]
        for copy in kv_copies(chunk):
            copy.start()

    for load in loads:
        load.wait()

    def gather(i, _):
        @pl.when(i < CX)
        def _():
            for way in (0, 1):
                x_copy(way, 1, i, 1).start()

        forward(x_copy, i, CX)

        @pl.when(i >= 4)
        def _():
            landed(x_copy, i, CX)
            project(i - 4)
        return 0

    lax.fori_loop(0, CX + 4, gather, 0)

    def kv_wait(chunk, _):
        rows = pl.ds(pl.multiple_of(chunk * RX, RX), RX)
        for dst in (0, 1, 2, 3, 5):
            pltpu.make_async_remote_copy(
                src_ref=kv.at[dst, rows], dst_ref=kv.at[dst, rows], send_sem=ks.at[0, chunk],
                recv_sem=kr.at[dst, chunk], device_id=sibling, device_id_type=MESH,
            ).wait_recv()
        return 0

    lax.fori_loop(0, CX, kv_wait, 0)

    def widen(n, _):
        rows = pl.ds(pl.multiple_of(n * SEG, SEG), SEG)
        wide[0, rows, :] = kv[n][:, :DH].astype(F32)
        wide[1, rows, :] = kv[n][:, DH:].astype(F32)
        return 0

    lax.fori_loop(0, 5, widen, 0)
    taps = cw_ref[:, :, columns].astype(F32)
    for u in range(2):
        for k in range(2):
            mixed = taps[0, k][None, :] * wide[k, pl.ds(1024 * u, SEG, 3), :]
            for r in (1, 2):
                mixed += taps[r, k][None, :] * wide[k, pl.ds(1024 * u + r, SEG, 3), :]
            comp[u, k] = mixed.astype(BF16)

    def attend(u, chunk):
        start = pl.multiple_of(chunk * RC, RC)
        rows = pl.ds(start, RC)
        q = qb[u, rows, :]
        gap = jnp.float32(-1e30)
        no_comp = jnp.where(block >= 1, jnp.float32(0), gap)
        no_mem = jnp.where(block * 4 + core + 2 * u >= 1, jnp.float32(0), gap)
        s_comp = lax.dot_general(q, comp[u, 0], NT, preferred_element_type=F32) + no_comp
        s_mem = lax.dot_general(q, kv[3 + 2 * u, :, :DH], NT, preferred_element_type=F32) + no_mem
        s_own = lax.dot_general(q, kv[4 + 2 * u, :, :DH], NT, preferred_element_type=F32)
        q_pos = start + lax.broadcasted_iota(jnp.int32, (RC, SEG), 0)
        k_pos = lax.broadcasted_iota(jnp.int32, (RC, SEG), 1)
        s_own = jnp.where(k_pos <= q_pos, s_own, gap)
        top = jnp.max(jnp.maximum(jnp.maximum(s_comp, s_mem), s_own), axis=-1, keepdims=True)
        e_comp = jnp.exp2((s_comp - top) * SCALE)
        e_mem = jnp.exp2((s_mem - top) * SCALE)
        e_own = jnp.exp2((s_own - top) * SCALE)
        norm = jnp.sum(e_comp + e_mem + e_own, axis=-1, keepdims=True)
        mixed = dot(e_comp.astype(BF16), comp[u, 1])
        mixed += dot(e_mem.astype(BF16), kv[3 + 2 * u, :, DH:])
        mixed += dot(e_own.astype(BF16), kv[4 + 2 * u, :, DH:])
        cb[y, u, rows, :] = (mixed / norm).astype(BF16)

    def share(i, _):
        @pl.when(i < CC)
        def _():
            for u in range(2):
                attend(u, i)
            for way in (0, 1):
                c_copy(way, 1, i, 1).start()

        forward(c_copy, i, CC)

        @pl.when(i >= 4)
        def _():
            landed(c_copy, i, CC)
        return 0

    lax.fori_loop(0, CC + 4, share, 0)

    stores = []
    for slot in range(RING):
        head = 2 * (slot % 4) + slot // 4
        store = pltpu.make_async_copy(
            cb.at[slot, hi], o_hbm.at[:, pl.ds(head * DH, DH)], lsem.at[4 + slot]
        )
        store.start()
        stores.append(store)

    def sent(chunk, _):
        for way in (0, 1):
            for dist in (1, 2, 3, 4):
                x_copy(way, dist, chunk, 1).wait_send()
                c_copy(way, dist, chunk, 1).wait_send()
        for copy in kv_copies(chunk):
            copy.wait_send()
        return 0

    lax.fori_loop(0, CX, sent, 0)
    for store in stores:
        store.wait()


def local(layer_input, w_qkv, comp_weight, w_out, n_seg):
    whole_out = lax.all_gather(w_out, "seg", axis=0, tiled=True)
    w = jnp.transpose(w_qkv, (1, 0, 2))
    any_spec = pl.BlockSpec(memory_space=pl.ANY)
    vmem_spec = pl.BlockSpec(memory_space=pltpu.VMEM)
    context = pl.pallas_call(
        functools.partial(kernel, n_seg),
        out_shape=jax.ShapeDtypeStruct((SEG, RING * DH), BF16),
        in_specs=[any_spec, any_spec, vmem_spec],
        out_specs=any_spec,
        scratch_shapes=[
            pltpu.VMEM((RING, SEG, FEAT), BF16),
            pltpu.VMEM((4 * FEAT, 3 * DH), BF16),
            pltpu.VMEM((7, SEG, 2 * DH), BF16),
            pltpu.VMEM((2, 5 * SEG + 8, DH), F32),
            pltpu.VMEM((2, 2, SEG, DH), BF16),
            pltpu.VMEM((2 * RX, 4 * FEAT), BF16),
            pltpu.VMEM((2, SEG, DH), BF16),
            pltpu.VMEM((RING, 2, SEG, DH), BF16),
            pltpu.SemaphoreType.DMA((12,)),
            pltpu.SemaphoreType.DMA((2, 4, CX)),
            pltpu.SemaphoreType.DMA((2, 4, CX)),
            pltpu.SemaphoreType.DMA((5, CX)),
            pltpu.SemaphoreType.DMA((7, CX)),
            pltpu.SemaphoreType.DMA((2, 4, CC)),
            pltpu.SemaphoreType.DMA((2, 4, CC)),
        ],
        compiler_params=pltpu.CompilerParams(
            collective_id=0, has_side_effects=True, vmem_limit_bytes=48 << 20
        ),
        cost_estimate=pl.CostEstimate(
            flops=3 * 10**9, bytes_accessed=200 * 10**6, transcendentals=2 * 10**6
        ),
        name="ring_layer",
    )(layer_input[0], w, comp_weight)
    out = jnp.dot(context, whole_out, preferred_element_type=F32)
    return out.astype(BF16)[None]


def solution(mesh):
    return jax.shard_map(
        functools.partial(local, n_seg=mesh.shape["seg"]),
        mesh=mesh,
        in_specs=(
            P(None, "seg", "head"),
            P(None, None, "head"),
            P(None, None, "head"),
            P("seg", "head"),
        ),
        out_specs=P(None, "seg", "head"),
        check_vma=False,
    )
```

```python
import functools
import math

import jax
import jax.numpy as jnp
from jax import lax
from jax.experimental import pallas as pl
from jax.experimental.pallas import tpu as pltpu
from jax.sharding import PartitionSpec as P

MESH = pl.DeviceIdType.MESH
F32, BF16 = jnp.float32, jnp.bfloat16
DH = 128
RING = 8
SEG = 512
FEAT = 512
CX = 8
RX = SEG // CX
CC = 4
LAG = 2
WZ = 5
RC = SEG // CC
SCALE = math.log2(math.e) / math.sqrt(DH)
NT = (((1,), (1,)), ((), ()))


def dot(a, b):
    return jnp.dot(a, b, preferred_element_type=F32)


def kernel(n_seg, x_hbm, w_hbm, cw_hbm, wo_hbm, o_ref, xb, wb, cw, w8, wo, kv, wide, comp, nb, qb,
           cb, lsem, xs, xr, ks, kr, cs, cr, ws, wr, kv_ready, z_ready):
    seg, lo = lax.axis_index("seg"), lax.axis_index("head")
    core, hi, block = seg % 2, (seg // 2) % 2, seg // 4
    y = hi * 4 + lo
    n_block = n_seg // 4

    def on_ring(pos):
        return (block * 4 + (pos // 4) * 2 + core, pos % 4)

    up, down = on_ring((y + 1) % RING), on_ring((y + RING - 1) % RING)
    sibling = (block * 4 + hi * 2 + 1 - core, lo)
    after, before = (block + 1) % n_block, (block + n_block - 1) % n_block
    after_same = (after * 4 + hi * 2 + core, lo)
    after_cross = (after * 4 + hi * 2 + 1 - core, lo)
    before_same = (before * 4 + hi * 2 + core, lo)
    before_cross = (before * 4 + hi * 2 + 1 - core, lo)

    zed, ex = block // 4, block % 4
    n_zed = n_block // 4
    across = (block * 4 + (1 - hi) * 2 + core, lo)
    rows_x = [((zed * 4 + (ex + d) % 4) * 4 + hi * 2 + core, lo) for d in range(1, 4)]
    rows_z = [((((zed + d) % n_zed) * 4 + ex) * 4 + hi * 2 + core, lo) for d in range(1, n_zed)]

    own = pltpu.make_async_copy(x_hbm, xb.at[y], lsem.at[0])
    own.start()
    own_out = pltpu.make_async_copy(wo_hbm, w8.at[core], lsem.at[4])
    own_out.start()
    taps_in = pltpu.make_async_copy(cw_hbm, cw, lsem.at[5])
    taps_in.start()
    columns = pl.ds(pl.multiple_of(hi * DH, DH), DH)
    loads = []
    for i in range(3):
        load = pltpu.make_async_copy(
            w_hbm.at[i, :, columns], wb.at[:, pl.ds(i * DH, DH)], lsem.at[1 + i]
        )
        load.start()
        loads.append(load)

    has_before, has_after = block > 0, block < n_block - 1

    @pl.when(block == 0)
    def _():
        kv[0:4] = jnp.zeros((4, SEG, 2 * DH), BF16)

    barrier = pltpu.get_barrier_semaphore()

    def signal(sem, device):
        pl.semaphore_signal(sem, inc=1, device_id=device, device_id_type=MESH)

    near = (up, down, sibling, across, *rows_x)
    for device in near:
        signal(barrier, device)

    @pl.when(has_after)
    def _():
        for device in (after_same, after_cross):
            signal(barrier, device)

    for d, device in enumerate(rows_z, 1):
        pl.when(zed + d < n_zed)(functools.partial(signal, barrier, device))
    pl.semaphore_wait(barrier, len(near) + zed + jnp.where(has_before, 2, 0))

    @pl.when(has_before)
    def _():
        for device in (before_same, before_cross):
            signal(kv_ready, device)

    for d, device in enumerate(rows_z, 1):
        pl.when(zed + d >= n_zed)(functools.partial(signal, z_ready, device))
    own.wait()
    own_out.wait()

    def out_copy(n, hop):
        back = 1 - hop
        if n == 0:
            at, device = w8.at[core if hop else 1 - core], sibling
        elif n == 1:
            start = (block * 2 + (hi if hop else 1 - hi)) * 16
            at, device = wo.at[pl.ds(pl.multiple_of(start, 16), 16)], across
        elif n < 5:
            d = n - 1
            start = (zed * 4 + (ex + 4 - d * back) % 4) * 32
            at, device = wo.at[pl.ds(pl.multiple_of(start, 32), 32)], rows_x[d - 1]
        else:
            d = (n - 5) % (n_zed - 1) + 1
            if n < 4 + n_zed:
                start = ((zed + n_zed - d * back) % n_zed) * 128 + core * 64
                device = rows_z[d - 1]
            else:
                start = ((zed + n_zed - d) % n_zed) * 128 + (core if hop else 1 - core) * 64
                device = sibling
            at = wo.at[pl.ds(pl.multiple_of(start, 64), 64)]
        return pltpu.make_async_remote_copy(
            src_ref=at, dst_ref=at, send_sem=ws.at[n], recv_sem=wr.at[n],
            device_id=device, device_id_type=MESH,
        )

    out_steps, z_end = 3 + 2 * n_zed, 4 + n_zed
    out_copy(0, 1).start()

    def gather_out(i):
        @pl.when(i == 1)
        def _():
            out_copy(0, 0).wait_recv()
            pair = jnp.concatenate([w8[0].astype(F32), w8[1].astype(F32)], axis=0)
            wo[pl.ds(pl.multiple_of((block * 2 + hi) * 16, 16), 16), :] = pair.astype(BF16)
            out_copy(1, 1).start()

        @pl.when(i == 2)
        def _():
            out_copy(1, 0).wait_recv()
            for n in range(2, 5):
                out_copy(n, 1).start()

        @pl.when(i == WZ)
        def _():
            for n in range(2, 5):
                out_copy(n, 0).wait_recv()

            @pl.when(zed < n_zed - 1)
            def _():
                pl.semaphore_wait(z_ready, n_zed - 1 - zed)

            for n in range(5, z_end):
                out_copy(n, 1).start()

        @pl.when(i == CX + 4 * LAG - 3)
        def _():
            for n in range(5, z_end):
                out_copy(n, 0).wait_recv()
                out_copy(n + n_zed - 1, 1).start()

    def ring_copy(view, ssem, rsem, way, dist, chunk, hop):
        step = dist - hop
        slot = (y + RING - step) % RING if way == 0 else (y + step) % RING
        ref = view(slot, way, dist, chunk, hop)
        return pltpu.make_async_remote_copy(
            src_ref=ref,
            dst_ref=ref,
            send_sem=ssem.at[way, dist - 1, chunk],
            recv_sem=rsem.at[way, dist - 1, chunk],
            device_id=up if way == 0 else down,
            device_id_type=MESH,
        )

    def x_view(slot, way, dist, chunk, hop):
        if dist < 4:
            return xb.at[slot, pl.ds(pl.multiple_of(chunk * RX, RX), RX)]
        half = RX // 2
        return xb.at[slot, pl.ds(pl.multiple_of(chunk * RX + way * half, half), half)]

    def c_view(slot, way, dist, chunk, hop):
        if dist < 4:
            return cb.at[slot, :, pl.ds(pl.multiple_of(chunk * RC, RC), RC)]
        half = RC // 2
        unit = 1 - slot // 4
        return cb.at[slot, unit, pl.ds(pl.multiple_of(chunk * RC + way * half, half), half)]

    x_copy = functools.partial(ring_copy, x_view, xs, xr)
    c_copy = functools.partial(ring_copy, c_view, cs, cr)

    def forward(copy, i, count):
        for dist in (1, 2, 3):
            @pl.when((i >= dist * LAG) & (i < count + dist * LAG))
            def _(dist=dist):
                for way in (0, 1):
                    copy(way, dist, i - dist * LAG, 0).wait_recv()
                    copy(way, dist + 1, i - dist * LAG, 1).start()

    def landed(copy, i, count):
        for way in (0, 1):
            copy(way, 4, i - 4 * LAG, 0).wait_recv()

    def kv_copies(chunk):
        rows = pl.ds(pl.multiple_of(chunk * RX, RX), RX)
        first_core = core == 0
        plan = (
            (4, jnp.where(first_core, 3, 5), sibling),
            (jnp.where(first_core, 6, 4), jnp.where(first_core, 5, 1),
             (jnp.where(first_core, sibling[0], after_cross[0]), lo)),
            (4, 0, after_same),
            (6, 2, after_same),
            (6, jnp.where(first_core, 1, 3), after_cross),
        )
        return [
            pltpu.make_async_remote_copy(
                src_ref=kv.at[src, rows],
                dst_ref=kv.at[dst, rows],
                send_sem=ks.at[n, chunk],
                recv_sem=kr.at[dst, chunk],
                device_id=device,
                device_id_type=MESH,
            )
            for n, (src, dst, device) in enumerate(plan)
        ]

    kv_sent = (True, (core == 0) | has_after, has_after, has_after, has_after)
    kv_received = ((5, True), (3, (core == 1) | has_before), (0, has_before), (1, has_before), (2, has_before))

    def project(chunk):
        rows = pl.ds(pl.multiple_of(chunk * RX, RX), RX)
        for u in range(2):
            parts = [xb[4 * u + f, rows, :].astype(F32) for f in range(4)]
            total = parts[0] + parts[1] + parts[2] + parts[3]
            mean = jnp.sum(total, axis=-1, keepdims=True) / (4 * FEAT)
            parts = [p - mean for p in parts]
            square = sum(p * p for p in parts[1:]) + parts[0] * parts[0]
            var = jnp.sum(square, axis=-1, keepdims=True) / (4 * FEAT)
            rstd = lax.rsqrt(var + 1e-05)
            for f in range(4):
                nb[u * RX:(u + 1) * RX, f * FEAT:(f + 1) * FEAT] = (parts[f] * rstd).astype(BF16)
        out = dot(nb[...], wb[...]).astype(BF16)
        for u in range(2):
            part = out[u * RX:(u + 1) * RX]
            qb[u, rows, :] = part[:, :DH]
            kv[4 + 2 * u, rows, :] = part[:, DH:]
        for copy, needed in zip(kv_copies(chunk), kv_sent):
            pl.when(needed)(copy.start)

    for load in loads:
        load.wait()

    def gather(i, _):
        @pl.when(i < CX)
        def _():
            for way in (0, 1):
                x_copy(way, 1, i, 1).start()

        forward(x_copy, i, CX)
        gather_out(i)

        @pl.when(i >= 4 * LAG)
        def _():
            landed(x_copy, i, CX)

            @pl.when((i == 4 * LAG) & has_after)
            def _():
                pl.semaphore_wait(kv_ready, 2)

            project(i - 4 * LAG)
        return 0

    lax.fori_loop(0, CX + 4 * LAG, gather, 0)

    def kv_wait(chunk, _):
        rows = pl.ds(pl.multiple_of(chunk * RX, RX), RX)
        for dst, needed in kv_received:
            copy = pltpu.make_async_remote_copy(
                src_ref=kv.at[dst, rows], dst_ref=kv.at[dst, rows], send_sem=ks.at[0, chunk],
                recv_sem=kr.at[dst, chunk], device_id=sibling, device_id_type=MESH,
            )
            pl.when(needed)(copy.wait_recv)
        return 0

    lax.fori_loop(0, CX, kv_wait, 0)

    def widen(n, _):
        rows = pl.ds(pl.multiple_of(n * SEG, SEG), SEG)
        wide[0, rows, :] = kv[n][:, :DH].astype(F32)
        wide[1, rows, :] = kv[n][:, DH:].astype(F32)
        return 0

    lax.fori_loop(0, 5, widen, 0)
    taps_in.wait()
    taps = cw[:, :, columns].astype(F32)
    for u in range(2):
        for k in range(2):
            mixed = taps[0, k][None, :] * wide[k, pl.ds(1024 * u, SEG, 3), :]
            for r in (1, 2):
                mixed += taps[r, k][None, :] * wide[k, pl.ds(1024 * u + r, SEG, 3), :]
            comp[u, k] = mixed.astype(BF16)

    def attend(u, chunk):
        start = pl.multiple_of(chunk * RC, RC)
        rows = pl.ds(start, RC)
        q = qb[u, rows, :]
        gap = jnp.float32(-1e30)
        no_comp = jnp.where(block >= 1, jnp.float32(0), gap)
        no_mem = jnp.where(block * 4 + core + 2 * u >= 1, jnp.float32(0), gap)
        s_comp = lax.dot_general(q, comp[u, 0], NT, preferred_element_type=F32) + no_comp
        s_mem = lax.dot_general(q, kv[3 + 2 * u, :, :DH], NT, preferred_element_type=F32) + no_mem
        s_own = lax.dot_general(q, kv[4 + 2 * u, :, :DH], NT, preferred_element_type=F32)
        q_pos = start + lax.broadcasted_iota(jnp.int32, (RC, SEG), 0)
        k_pos = lax.broadcasted_iota(jnp.int32, (RC, SEG), 1)
        s_own = jnp.where(k_pos <= q_pos, s_own, gap)
        top = jnp.max(jnp.maximum(jnp.maximum(s_comp, s_mem), s_own), axis=-1, keepdims=True)
        e_comp = jnp.exp2((s_comp - top) * SCALE)
        e_mem = jnp.exp2((s_mem - top) * SCALE)
        e_own = jnp.exp2((s_own - top) * SCALE)
        norm = jnp.sum(e_comp + e_mem + e_own, axis=-1, keepdims=True)
        mixed = dot(e_comp.astype(BF16), comp[u, 1])
        mixed += dot(e_mem.astype(BF16), kv[3 + 2 * u, :, DH:])
        mixed += dot(e_own.astype(BF16), kv[4 + 2 * u, :, DH:])
        cb[y, u, rows, :] = (mixed / norm).astype(BF16)

    def share(i, _):
        @pl.when(i < CC)
        def _():
            for u in range(2):
                attend(u, i)
            for way in (0, 1):
                c_copy(way, 1, i, 1).start()

        forward(c_copy, i, CC)

        @pl.when(i >= 4 * LAG)
        def _():
            landed(c_copy, i, CC)
            rows = pl.ds(pl.multiple_of((i - 4 * LAG) * RC, RC), RC)
            whole = jnp.concatenate([cb[slot, hi, rows, :] for slot in (0, 4, 1, 5, 2, 6, 3, 7)], axis=1)
            o_ref[rows, :] = dot(whole, wo[...]).astype(BF16)
        return 0

    for n in range(z_end, out_steps):
        out_copy(n, 0).wait_recv()
    lax.fori_loop(0, CC + 4 * LAG, share, 0)

    def sent(chunk, _):
        for way in (0, 1):
            for dist in (1, 2, 3, 4):
                x_copy(way, dist, chunk, 1).wait_send()
        for copy, needed in zip(kv_copies(chunk), kv_sent):
            pl.when(needed)(copy.wait_send)
        return 0

    lax.fori_loop(0, CX, sent, 0)

    def c_sent(chunk, _):
        for way in (0, 1):
            for dist in (1, 2, 3, 4):
                c_copy(way, dist, chunk, 1).wait_send()
        return 0

    lax.fori_loop(0, CC, c_sent, 0)
    for n in range(out_steps):
        out_copy(n, 1).wait_send()


def local(layer_input, w_qkv, comp_weight, w_out, n_seg):
    w = jnp.transpose(w_qkv, (1, 0, 2))
    any_spec = pl.BlockSpec(memory_space=pl.ANY)
    out = pl.pallas_call(
        functools.partial(kernel, n_seg),
        out_shape=jax.ShapeDtypeStruct((SEG, FEAT), BF16),
        in_specs=[any_spec] * 4,
        out_specs=pl.BlockSpec(memory_space=pltpu.VMEM),
        scratch_shapes=[
            pltpu.VMEM((RING, SEG, FEAT), BF16),
            pltpu.VMEM((4 * FEAT, 3 * DH), BF16),
            pltpu.VMEM((3, 2, 2 * DH), BF16),
            pltpu.VMEM((2, 8, FEAT), BF16),
            pltpu.VMEM((RING * DH, FEAT), BF16),
            pltpu.VMEM((7, SEG, 2 * DH), BF16),
            pltpu.VMEM((2, 5 * SEG + 8, DH), F32),
            pltpu.VMEM((2, 2, SEG, DH), BF16),
            pltpu.VMEM((2 * RX, 4 * FEAT), BF16),
            pltpu.VMEM((2, SEG, DH), BF16),
            pltpu.VMEM((RING, 2, SEG, DH), BF16),
            pltpu.SemaphoreType.DMA((6,)),
            pltpu.SemaphoreType.DMA((2, 4, CX)),
            pltpu.SemaphoreType.DMA((2, 4, CX)),
            pltpu.SemaphoreType.DMA((5, CX)),
            pltpu.SemaphoreType.DMA((7, CX)),
            pltpu.SemaphoreType.DMA((2, 4, CC)),
            pltpu.SemaphoreType.DMA((2, 4, CC)),
            pltpu.SemaphoreType.DMA((3 + n_seg // 8,)),
            pltpu.SemaphoreType.DMA((3 + n_seg // 8,)),
            pltpu.SemaphoreType.REGULAR,
            pltpu.SemaphoreType.REGULAR,
        ],
        compiler_params=pltpu.CompilerParams(
            collective_id=0, has_side_effects=True, vmem_limit_bytes=60 << 20
        ),
        cost_estimate=pl.CostEstimate(
            flops=3 * 10**9, bytes_accessed=200 * 10**6, transcendentals=2 * 10**6
        ),
        name="ring_layer",
    )(layer_input[0], w, comp_weight, w_out)
    return out[None]


def solution(mesh):
    return jax.shard_map(
        functools.partial(local, n_seg=mesh.shape["seg"]),
        mesh=mesh,
        in_specs=(
            P(None, "seg", "head"),
            P(None, None, "head"),
            P(None, None, "head"),
            P("seg", "head"),
        ),
        out_specs=P(None, "seg", "head"),
        check_vma=False,
    )
```

```python
import functools
import math

import jax
import jax.numpy as jnp
from jax import lax
from jax.experimental import pallas as pl
from jax.experimental.pallas import tpu as pltpu
from jax.sharding import PartitionSpec as P

MESH = pl.DeviceIdType.MESH
F32, BF16 = jnp.float32, jnp.bfloat16
DH = 128
RING = 8
SEG = 512
FEAT = 512
CX = 8
RX = SEG // CX
CC = 4
LAG = 2
LAGC = 3
WZ = 6
RC = SEG // CC
SCALE = math.log2(math.e) / math.sqrt(DH)
NT = (((1,), (1,)), ((), ()))


def when(needed, act):
    if needed is True:
        act()
    else:
        pl.when(needed)(act)


def dot(a, b):
    return jnp.dot(a, b, preferred_element_type=F32)


def kernel(n_seg, x_hbm, w_hbm, cw_hbm, wo_hbm, o_ref, xb, wb, cw, w8, wo, kv, wide, comp, nb, qb,
           cb, lsem, xs, xr, ks, kr, cs, cr, ws, wr, kv_ready, z_ready):
    seg, lo = lax.axis_index("seg"), lax.axis_index("head")
    core, hi, block = seg % 2, (seg // 2) % 2, seg // 4
    y = hi * 4 + lo
    n_block = n_seg // 4

    def on_ring(pos):
        return (block * 4 + (pos // 4) * 2 + core, pos % 4)

    up, down = on_ring((y + 1) % RING), on_ring((y + RING - 1) % RING)
    sibling = (block * 4 + hi * 2 + 1 - core, lo)
    after = (((block + 1) % n_block) * 4 + hi * 2 + core, lo)
    before = (((block + n_block - 1) % n_block) * 4 + hi * 2 + core, lo)

    zed, ex = block // 4, block % 4
    n_zed = n_block // 4
    across = (block * 4 + (1 - hi) * 2 + core, lo)
    rows_x = [((zed * 4 + (ex + d) % 4) * 4 + hi * 2 + core, lo) for d in range(1, 4)]
    rows_z = [((((zed + d) % n_zed) * 4 + ex) * 4 + hi * 2 + core, lo) for d in range(1, n_zed)]

    own = pltpu.make_async_copy(x_hbm, xb.at[y], lsem.at[0])
    own.start()
    own_out = pltpu.make_async_copy(wo_hbm, w8.at[core], lsem.at[4])
    own_out.start()
    taps_in = pltpu.make_async_copy(cw_hbm, cw, lsem.at[5])
    taps_in.start()
    columns = pl.ds(pl.multiple_of(hi * DH, DH), DH)
    loads = []
    for i in range(3):
        load = pltpu.make_async_copy(
            w_hbm.at[i, :, columns], wb.at[:, pl.ds(i * DH, DH)], lsem.at[1 + i]
        )
        load.start()
        loads.append(load)

    has_before, has_after = block > 0, block < n_block - 1

    @pl.when(block == 0)
    def _():
        kv[0:4] = jnp.zeros((4, SEG, 2 * DH), BF16)

    barrier = pltpu.get_barrier_semaphore()

    def signal(sem, device):
        pl.semaphore_signal(sem, inc=1, device_id=device, device_id_type=MESH)

    near = (up, down, sibling, across, *rows_x)
    for device in near:
        signal(barrier, device)

    pl.when(has_after)(functools.partial(signal, barrier, after))
    for d, device in enumerate(rows_z, 1):
        pl.when(zed + d < n_zed)(functools.partial(signal, barrier, device))
    pl.semaphore_wait(barrier, len(near) + zed + jnp.where(has_before, 1, 0))

    pl.when(has_before)(functools.partial(signal, kv_ready, before))
    for d, device in enumerate(rows_z, 1):
        pl.when(zed + d >= n_zed)(functools.partial(signal, z_ready, device))

    def out_copy(n, hop):
        back = 1 - hop
        if n == 0:
            at, device = w8.at[core if hop else 1 - core], sibling
        elif n == 1:
            start = (block * 2 + (hi if hop else 1 - hi)) * 16
            at, device = wo.at[pl.ds(pl.multiple_of(start, 16), 16)], across
        elif n < 5:
            d = n - 1
            start = (zed * 4 + (ex + 4 - d * back) % 4) * 32
            at, device = wo.at[pl.ds(pl.multiple_of(start, 32), 32)], rows_x[d - 1]
        else:
            d = (n - 5) % (n_zed - 1) + 1
            if n < 4 + n_zed:
                start = ((zed + n_zed - d * back) % n_zed) * 128 + core * 64
                device = rows_z[d - 1]
            else:
                start = ((zed + n_zed - d) % n_zed) * 128 + (core if hop else 1 - core) * 64
                device = sibling
            at = wo.at[pl.ds(pl.multiple_of(start, 64), 64)]
        return pltpu.make_async_remote_copy(
            src_ref=at, dst_ref=at, send_sem=ws.at[n], recv_sem=wr.at[n],
            device_id=device, device_id_type=MESH,
        )

    out_steps, z_end = 3 + 2 * n_zed, 4 + n_zed

    def gather_out(i):
        @pl.when(i == 0)
        def _():
            own_out.wait()
            out_copy(0, 1).start()

        @pl.when(i == 1)
        def _():
            out_copy(0, 0).wait_recv()
            pair = jnp.concatenate([w8[0].astype(F32), w8[1].astype(F32)], axis=0)
            wo[pl.ds(pl.multiple_of((block * 2 + hi) * 16, 16), 16), :] = pair.astype(BF16)
            out_copy(1, 1).start()

        @pl.when(i == 3)
        def _():
            out_copy(1, 0).wait_recv()
            for n in range(2, 5):
                out_copy(n, 1).start()

        @pl.when(i == WZ)
        def _():
            for n in range(2, 5):
                out_copy(n, 0).wait_recv()

            @pl.when(zed < n_zed - 1)
            def _():
                pl.semaphore_wait(z_ready, n_zed - 1 - zed)

            for n in range(5, z_end):
                out_copy(n, 1).start()


    def ring_copy(view, ssem, rsem, way, dist, chunk, hop):
        step = dist - hop
        slot = (y + RING - step) % RING if way == 0 else (y + step) % RING
        ref = view(slot, way, dist, chunk)
        return pltpu.make_async_remote_copy(
            src_ref=ref,
            dst_ref=ref,
            send_sem=ssem.at[way, dist - 1, chunk],
            recv_sem=rsem.at[way, dist - 1, chunk],
            device_id=up if way == 0 else down,
            device_id_type=MESH,
        )

    def x_view(slot, way, dist, chunk):
        if dist < 4:
            return xb.at[slot, pl.ds(pl.multiple_of(chunk * RX, RX), RX)]
        half = RX // 2
        return xb.at[slot, pl.ds(pl.multiple_of(chunk * RX + way * half, half), half)]

    def c_view(slot, way, dist, chunk):
        if dist < 4:
            return cb.at[slot, :, pl.ds(pl.multiple_of(chunk * RC, RC), RC)]
        half = RC // 2
        unit = 1 - slot // 4
        return cb.at[slot, unit, pl.ds(pl.multiple_of(chunk * RC + way * half, half), half)]

    x_copy = functools.partial(ring_copy, x_view, xs, xr)
    c_copy = functools.partial(ring_copy, c_view, cs, cr)

    def forward(copy, i, count, lag=LAG):
        for dist in (1, 2, 3):
            @pl.when((i >= dist * lag) & (i < count + dist * lag))
            def _(dist=dist):
                for way in (0, 1):
                    copy(way, dist, i - dist * lag, 0).wait_recv()
                    copy(way, dist + 1, i - dist * lag, 1).start()

    def landed(copy, i, count, lag=LAG):
        for way in (0, 1):
            copy(way, 4, i - 4 * lag, 0).wait_recv()

    def kv_copies(chunk):
        rows = pl.ds(pl.multiple_of(chunk * RX, RX), RX)
        first_core = core == 0
        plan = (
            (4, jnp.where(first_core, 3, 5), sibling),
            (6, 5, sibling),
            (4, 0, after),
            (6, 2, after),
            (jnp.where(first_core, 2, 0), 1, sibling),
            (2, 3, sibling),
        )
        return [
            pltpu.make_async_remote_copy(
                src_ref=kv.at[src, rows],
                dst_ref=kv.at[dst, rows],
                send_sem=ks.at[n, chunk],
                recv_sem=kr.at[dst, chunk],
                device_id=device,
                device_id_type=MESH,
            )
            for n, (src, dst, device) in enumerate(plan)
        ]

    kv_sent = (True, core == 0, has_after, has_after, has_before, (core == 1) & has_before)
    kv_received = ((1, has_before), (3, (core == 1) | has_before), (5, True))

    def kv_landed(slots, chunk):
        rows = pl.ds(pl.multiple_of(chunk * RX, RX), RX)
        for dst, needed in slots:
            copy = pltpu.make_async_remote_copy(
                src_ref=kv.at[dst, rows], dst_ref=kv.at[dst, rows], send_sem=ks.at[0, chunk],
                recv_sem=kr.at[dst, chunk], device_id=sibling, device_id_type=MESH,
            )
            when(needed, copy.wait_recv)

    def relay(chunk):
        kv_landed(((0, has_before), (2, has_before)), chunk)
        for copy, needed in zip(kv_copies(chunk)[4:], kv_sent[4:]):
            when(needed, copy.start)

    def project(chunk):
        rows = pl.ds(pl.multiple_of(chunk * RX, RX), RX)
        for u in range(2):
            parts = [xb[4 * u + f, rows, :].astype(F32) for f in range(4)]
            total = parts[0] + parts[1] + parts[2] + parts[3]
            mean = jnp.sum(total, axis=-1, keepdims=True) / (4 * FEAT)
            parts = [p - mean for p in parts]
            square = sum(p * p for p in parts[1:]) + parts[0] * parts[0]
            var = jnp.sum(square, axis=-1, keepdims=True) / (4 * FEAT)
            rstd = lax.rsqrt(var + 1e-05)
            for f in range(4):
                nb[u * RX:(u + 1) * RX, f * FEAT:(f + 1) * FEAT] = (parts[f] * rstd).astype(BF16)
        out = dot(nb[...], wb[...]).astype(BF16)
        for u in range(2):
            part = out[u * RX:(u + 1) * RX]
            qb[u, rows, :] = part[:, :DH]
            kv[4 + 2 * u, rows, :] = part[:, DH:]
        for copy, needed in zip(kv_copies(chunk)[:4], kv_sent[:4]):
            when(needed, copy.start)

    own.wait()

    def gather(i, _):
        @pl.when(i < CX)
        def _():
            for way in (0, 1):
                x_copy(way, 1, i, 1).start()

        forward(x_copy, i, CX)
        gather_out(i)

        @pl.when(i == 3)
        def _():
            for load in loads:
                load.wait()

        @pl.when(i >= 4 * LAG)
        def _():
            landed(x_copy, i, CX)

            @pl.when((i == 4 * LAG) & has_after)
            def _():
                pl.semaphore_wait(kv_ready, 1)

            project(i - 4 * LAG)

            @pl.when(i >= 4 * LAG + 3)
            def _():
                relay(i - 4 * LAG - 3)
        return 0

    lax.fori_loop(0, CX + 4 * LAG, gather, 0)

    for chunk in range(CX - 3, CX):
        relay(chunk)

    for n in range(5, z_end):
        out_copy(n, 0).wait_recv()
        out_copy(n + n_zed - 1, 1).start()

    def kv_wait(chunk, _):
        kv_landed(kv_received, chunk)
        return 0

    lax.fori_loop(0, CX, kv_wait, 0)

    def widen(n, _):
        rows = pl.ds(pl.multiple_of(n * SEG, SEG), SEG)
        wide[0, rows, :] = kv[n][:, :DH].astype(F32)
        wide[1, rows, :] = kv[n][:, DH:].astype(F32)
        return 0

    lax.fori_loop(0, 5, widen, 0)
    taps_in.wait()
    taps = cw[:, :, columns].astype(F32)
    for u in range(2):
        for k in range(2):
            mixed = taps[0, k][None, :] * wide[k, pl.ds(1024 * u, SEG, 3), :]
            for r in (1, 2):
                mixed += taps[r, k][None, :] * wide[k, pl.ds(1024 * u + r, SEG, 3), :]
            comp[u, k] = mixed.astype(BF16)

    def attend(u, chunk):
        start = pl.multiple_of(chunk * RC, RC)
        rows = pl.ds(start, RC)
        q = qb[u, rows, :]
        gap = jnp.float32(-1e30)
        no_comp = jnp.where(block >= 1, jnp.float32(0), gap)
        no_mem = jnp.where(block * 4 + core + 2 * u >= 1, jnp.float32(0), gap)
        s_comp = lax.dot_general(q, comp[u, 0], NT, preferred_element_type=F32) + no_comp
        s_mem = lax.dot_general(q, kv[3 + 2 * u, :, :DH], NT, preferred_element_type=F32) + no_mem
        s_own = lax.dot_general(q, kv[4 + 2 * u, :, :DH], NT, preferred_element_type=F32)
        q_pos = start + lax.broadcasted_iota(jnp.int32, (RC, SEG), 0)
        k_pos = lax.broadcasted_iota(jnp.int32, (RC, SEG), 1)
        s_own = jnp.where(k_pos <= q_pos, s_own, gap)
        top = jnp.max(jnp.maximum(jnp.maximum(s_comp, s_mem), s_own), axis=-1, keepdims=True)
        e_comp = jnp.exp2((s_comp - top) * SCALE)
        e_mem = jnp.exp2((s_mem - top) * SCALE)
        e_own = jnp.exp2((s_own - top) * SCALE)
        norm = jnp.sum(e_comp + e_mem + e_own, axis=-1, keepdims=True)
        mixed = dot(e_comp.astype(BF16), comp[u, 1])
        mixed += dot(e_mem.astype(BF16), kv[3 + 2 * u, :, DH:])
        mixed += dot(e_own.astype(BF16), kv[4 + 2 * u, :, DH:])
        cb[y, u, rows, :] = (mixed / norm).astype(BF16)

    def share(i, _):
        @pl.when(i < CC)
        def _():
            for u in range(2):
                attend(u, i)
            for way in (0, 1):
                c_copy(way, 1, i, 1).start()

        forward(c_copy, i, CC, LAGC)

        @pl.when(i >= 4 * LAGC)
        def _():
            landed(c_copy, i, CC, LAGC)

            @pl.when(i == 4 * LAGC)
            def _():
                for n in range(z_end, out_steps):
                    out_copy(n, 0).wait_recv()

            rows = pl.ds(pl.multiple_of((i - 4 * LAGC) * RC, RC), RC)
            whole = jnp.concatenate([cb[slot, hi, rows, :] for slot in (0, 4, 1, 5, 2, 6, 3, 7)], axis=1)
            o_ref[rows, :] = dot(whole, wo[...]).astype(BF16)
        return 0

    lax.fori_loop(0, CC + 4 * LAGC, share, 0)

    def sent(chunk, _):
        for way in (0, 1):
            for dist in (1, 2, 3, 4):
                x_copy(way, dist, chunk, 1).wait_send()
        for copy, needed in zip(kv_copies(chunk), kv_sent):
            when(needed, copy.wait_send)
        return 0

    lax.fori_loop(0, CX, sent, 0)

    def c_sent(chunk, _):
        for way in (0, 1):
            for dist in (1, 2, 3, 4):
                c_copy(way, dist, chunk, 1).wait_send()
        return 0

    lax.fori_loop(0, CC, c_sent, 0)
    for n in range(out_steps):
        out_copy(n, 1).wait_send()


def local(layer_input, w_qkv, comp_weight, w_out, n_seg):
    w = jnp.transpose(w_qkv, (1, 0, 2))
    any_spec = pl.BlockSpec(memory_space=pl.ANY)
    out = pl.pallas_call(
        functools.partial(kernel, n_seg),
        out_shape=jax.ShapeDtypeStruct((SEG, FEAT), BF16),
        in_specs=[any_spec] * 4,
        out_specs=pl.BlockSpec(memory_space=pltpu.VMEM),
        scratch_shapes=[
            pltpu.VMEM((RING, SEG, FEAT), BF16),
            pltpu.VMEM((4 * FEAT, 3 * DH), BF16),
            pltpu.VMEM((3, 2, 2 * DH), BF16),
            pltpu.VMEM((2, 8, FEAT), BF16),
            pltpu.VMEM((RING * DH, FEAT), BF16),
            pltpu.VMEM((7, SEG, 2 * DH), BF16),
            pltpu.VMEM((2, 5 * SEG + 8, DH), F32),
            pltpu.VMEM((2, 2, SEG, DH), BF16),
            pltpu.VMEM((2 * RX, 4 * FEAT), BF16),
            pltpu.VMEM((2, SEG, DH), BF16),
            pltpu.VMEM((RING, 2, SEG, DH), BF16),
            pltpu.SemaphoreType.DMA((6,)),
            pltpu.SemaphoreType.DMA((2, 4, CX)),
            pltpu.SemaphoreType.DMA((2, 4, CX)),
            pltpu.SemaphoreType.DMA((6, CX)),
            pltpu.SemaphoreType.DMA((7, CX)),
            pltpu.SemaphoreType.DMA((2, 4, CC)),
            pltpu.SemaphoreType.DMA((2, 4, CC)),
            pltpu.SemaphoreType.DMA((3 + n_seg // 8,)),
            pltpu.SemaphoreType.DMA((3 + n_seg // 8,)),
            pltpu.SemaphoreType.REGULAR,
            pltpu.SemaphoreType.REGULAR,
        ],
        compiler_params=pltpu.CompilerParams(
            collective_id=0, has_side_effects=True, vmem_limit_bytes=60 << 20
        ),
        cost_estimate=pl.CostEstimate(
            flops=3 * 10**9, bytes_accessed=200 * 10**6, transcendentals=2 * 10**6
        ),
        name="ring_layer",
    )(layer_input[0], w, comp_weight, w_out)
    return out[None]


def solution(mesh):
    return jax.shard_map(
        functools.partial(local, n_seg=mesh.shape["seg"]),
        mesh=mesh,
        in_specs=(
            P(None, "seg", "head"),
            P(None, None, "head"),
            P(None, None, "head"),
            P("seg", "head"),
        ),
        out_specs=P(None, "seg", "head"),
        check_vma=False,
    )
```

```python
import functools
import math

import jax
import jax.numpy as jnp
from jax import lax
from jax.experimental import pallas as pl
from jax.experimental.pallas import tpu as pltpu
from jax.sharding import PartitionSpec as P

MESH = pl.DeviceIdType.MESH
F32, BF16 = jnp.float32, jnp.bfloat16
DH = 128
RING = 8
SEG = 512
FEAT = 512
CX = 8
RX = SEG // CX
CC = 4
LAG = 2
LAGC = 3
WZ = 6
RC = SEG // CC
SCALE = math.log2(math.e) / math.sqrt(DH)
NT = (((1,), (1,)), ((), ()))


def when(needed, act):
    if needed is True:
        act()
    else:
        pl.when(needed)(act)


def dot(a, b):
    return jnp.dot(a, b, preferred_element_type=F32)


def kernel(n_seg, x_hbm, w_hbm, cw_hbm, wo_hbm, o_ref, xb, wb, cw, w8, wo, kv, wide, comp, nb, qb,
           cb, lsem, xs, xr, ks, kr, cs, cr, ws, wr, kv_ready, z_ready, x_ready, y_ready):
    seg, lo = lax.axis_index("seg"), lax.axis_index("head")
    core, hi, block = seg % 2, (seg // 2) % 2, seg // 4
    y = hi * 4 + lo
    n_block = n_seg // 4

    def on_ring(pos):
        return (block * 4 + (pos // 4) * 2 + core, pos % 4)

    up, down = on_ring((y + 1) % RING), on_ring((y + RING - 1) % RING)
    sibling = (block * 4 + hi * 2 + 1 - core, lo)
    after = (((block + 1) % n_block) * 4 + hi * 2 + core, lo)
    before = (((block + n_block - 1) % n_block) * 4 + hi * 2 + core, lo)

    zed, ex = block // 4, block % 4
    n_zed = n_block // 4
    across = (block * 4 + (1 - hi) * 2 + core, lo)
    rows_x = [((zed * 4 + (ex + d) % 4) * 4 + hi * 2 + core, lo) for d in range(1, 4)]
    rows_z = [((((zed + d) % n_zed) * 4 + ex) * 4 + hi * 2 + core, lo) for d in range(1, n_zed)]

    own = pltpu.make_async_copy(x_hbm, xb.at[y], lsem.at[0])
    own.start()
    own_out = pltpu.make_async_copy(wo_hbm, w8.at[core], lsem.at[4])
    own_out.start()
    taps_in = pltpu.make_async_copy(cw_hbm, cw, lsem.at[5])
    taps_in.start()
    columns = pl.ds(pl.multiple_of(hi * DH, DH), DH)
    loads = []
    for i in range(3):
        load = pltpu.make_async_copy(
            w_hbm.at[i, :, columns], wb.at[:, pl.ds(i * DH, DH)], lsem.at[1 + i]
        )
        load.start()
        loads.append(load)

    has_before, has_after = block > 0, block < n_block - 1

    @pl.when(block == 0)
    def _():
        kv[0:4] = jnp.zeros((4, SEG, 2 * DH), BF16)

    barrier = pltpu.get_barrier_semaphore()

    def signal(sem, device):
        pl.semaphore_signal(sem, inc=1, device_id=device, device_id_type=MESH)

    near = (up, down, sibling)
    for device in near:
        signal(barrier, device)

    pl.when(has_after)(functools.partial(signal, barrier, after))
    pl.when(hi == 0)(functools.partial(signal, barrier, across))
    for d, device in enumerate(rows_x, 1):
        pl.when(ex + d < 4)(functools.partial(signal, barrier, device))
    for d, device in enumerate(rows_z, 1):
        pl.when(zed + d < n_zed)(functools.partial(signal, barrier, device))
    pl.semaphore_wait(barrier, len(near) + zed + ex + hi + jnp.where(has_before, 1, 0))

    pl.when(has_before)(functools.partial(signal, kv_ready, before))
    pl.when(hi == 1)(functools.partial(signal, y_ready, across))
    for d, device in enumerate(rows_x, 1):
        pl.when(ex + d >= 4)(functools.partial(signal, x_ready, device))
    for d, device in enumerate(rows_z, 1):
        pl.when(zed + d >= n_zed)(functools.partial(signal, z_ready, device))

    def out_copy(n, hop):
        back = 1 - hop
        if n == 0:
            at, device = w8.at[core if hop else 1 - core], sibling
        elif n == 1:
            start = (block * 2 + (hi if hop else 1 - hi)) * 16
            at, device = wo.at[pl.ds(pl.multiple_of(start, 16), 16)], across
        elif n < 5:
            d = n - 1
            start = (zed * 4 + (ex + 4 - d * back) % 4) * 32
            at, device = wo.at[pl.ds(pl.multiple_of(start, 32), 32)], rows_x[d - 1]
        else:
            d = (n - 5) % (n_zed - 1) + 1
            if n < 4 + n_zed:
                start = ((zed + n_zed - d * back) % n_zed) * 128 + core * 64
                device = rows_z[d - 1]
            else:
                start = ((zed + n_zed - d) % n_zed) * 128 + (core if hop else 1 - core) * 64
                device = sibling
            at = wo.at[pl.ds(pl.multiple_of(start, 64), 64)]
        return pltpu.make_async_remote_copy(
            src_ref=at, dst_ref=at, send_sem=ws.at[n], recv_sem=wr.at[n],
            device_id=device, device_id_type=MESH,
        )

    out_steps, z_end = 3 + 2 * n_zed, 4 + n_zed

    def gather_out(i):
        @pl.when(i == 0)
        def _():
            own_out.wait()
            out_copy(0, 1).start()

        @pl.when(i == 2)
        def _():
            out_copy(0, 0).wait_recv()
            pair = jnp.concatenate([w8[0].astype(F32), w8[1].astype(F32)], axis=0)
            wo[pl.ds(pl.multiple_of((block * 2 + hi) * 16, 16), 16), :] = pair.astype(BF16)

            @pl.when(hi == 0)
            def _():
                pl.semaphore_wait(y_ready, 1)

            out_copy(1, 1).start()

        @pl.when(i == 4)
        def _():
            out_copy(1, 0).wait_recv()

            @pl.when(ex < 3)
            def _():
                pl.semaphore_wait(x_ready, 3 - ex)

            for n in range(2, 5):
                out_copy(n, 1).start()

        @pl.when(i == WZ)
        def _():
            for n in range(2, 5):
                out_copy(n, 0).wait_recv()

            @pl.when(zed < n_zed - 1)
            def _():
                pl.semaphore_wait(z_ready, n_zed - 1 - zed)

            for n in range(5, z_end):
                out_copy(n, 1).start()


    def ring_copy(view, ssem, rsem, way, dist, chunk, hop):
        step = dist - hop
        slot = (y + RING - step) % RING if way == 0 else (y + step) % RING
        ref = view(slot, way, dist, chunk)
        return pltpu.make_async_remote_copy(
            src_ref=ref,
            dst_ref=ref,
            send_sem=ssem.at[way, dist - 1, chunk],
            recv_sem=rsem.at[way, dist - 1, chunk],
            device_id=up if way == 0 else down,
            device_id_type=MESH,
        )

    def x_view(slot, way, dist, chunk):
        if dist < 4:
            return xb.at[slot, pl.ds(pl.multiple_of(chunk * RX, RX), RX)]
        half = RX // 2
        return xb.at[slot, pl.ds(pl.multiple_of(chunk * RX + way * half, half), half)]

    def c_view(slot, way, dist, chunk):
        if dist < 4:
            return cb.at[slot, :, pl.ds(pl.multiple_of(chunk * RC, RC), RC)]
        half = RC // 2
        unit = 1 - slot // 4
        return cb.at[slot, unit, pl.ds(pl.multiple_of(chunk * RC + way * half, half), half)]

    x_copy = functools.partial(ring_copy, x_view, xs, xr)
    c_copy = functools.partial(ring_copy, c_view, cs, cr)

    def forward(copy, i, count, lag=LAG):
        for dist in (1, 2, 3):
            @pl.when((i >= dist * lag) & (i < count + dist * lag))
            def _(dist=dist):
                for way in (0, 1):
                    copy(way, dist, i - dist * lag, 0).wait_recv()
                    copy(way, dist + 1, i - dist * lag, 1).start()

    def landed(copy, i, count, lag=LAG):
        for way in (0, 1):
            copy(way, 4, i - 4 * lag, 0).wait_recv()

    def kv_copies(chunk):
        rows = pl.ds(pl.multiple_of(chunk * RX, RX), RX)
        first_core = core == 0
        plan = (
            (4, jnp.where(first_core, 3, 5), sibling),
            (6, 5, sibling),
            (4, 0, after),
            (6, 2, after),
            (jnp.where(first_core, 2, 0), 1, sibling),
            (2, 3, sibling),
        )
        return [
            pltpu.make_async_remote_copy(
                src_ref=kv.at[src, rows],
                dst_ref=kv.at[dst, rows],
                send_sem=ks.at[n, chunk],
                recv_sem=kr.at[dst, chunk],
                device_id=device,
                device_id_type=MESH,
            )
            for n, (src, dst, device) in enumerate(plan)
        ]

    kv_sent = (True, core == 0, has_after, has_after, has_before, (core == 1) & has_before)
    kv_received = ((1, has_before), (3, (core == 1) | has_before), (5, True))

    def kv_landed(slots, chunk):
        rows = pl.ds(pl.multiple_of(chunk * RX, RX), RX)
        for dst, needed in slots:
            copy = pltpu.make_async_remote_copy(
                src_ref=kv.at[dst, rows], dst_ref=kv.at[dst, rows], send_sem=ks.at[0, chunk],
                recv_sem=kr.at[dst, chunk], device_id=sibling, device_id_type=MESH,
            )
            when(needed, copy.wait_recv)

    def relay(chunk):
        kv_landed(((0, has_before), (2, has_before)), chunk)
        for copy, needed in zip(kv_copies(chunk)[4:], kv_sent[4:]):
            when(needed, copy.start)

    def project(chunk):
        rows = pl.ds(pl.multiple_of(chunk * RX, RX), RX)
        for u in range(2):
            parts = [xb[4 * u + f, rows, :].astype(F32) for f in range(4)]
            total = parts[0] + parts[1] + parts[2] + parts[3]
            mean = jnp.sum(total, axis=-1, keepdims=True) / (4 * FEAT)
            parts = [p - mean for p in parts]
            square = sum(p * p for p in parts[1:]) + parts[0] * parts[0]
            var = jnp.sum(square, axis=-1, keepdims=True) / (4 * FEAT)
            rstd = lax.rsqrt(var + 1e-05)
            for f in range(4):
                nb[u * RX:(u + 1) * RX, f * FEAT:(f + 1) * FEAT] = (parts[f] * rstd).astype(BF16)
        out = dot(nb[...], wb[...]).astype(BF16)
        for u in range(2):
            part = out[u * RX:(u + 1) * RX]
            qb[u, rows, :] = part[:, :DH]
            kv[4 + 2 * u, rows, :] = part[:, DH:]
        for copy, needed in zip(kv_copies(chunk)[:4], kv_sent[:4]):
            when(needed, copy.start)

    own.wait()

    def gather(i, _):
        @pl.when(i < CX)
        def _():
            for way in (0, 1):
                x_copy(way, 1, i, 1).start()

        forward(x_copy, i, CX)
        gather_out(i)

        @pl.when(i == 3)
        def _():
            for load in loads:
                load.wait()

        @pl.when(i >= 4 * LAG)
        def _():
            landed(x_copy, i, CX)

            @pl.when((i == 4 * LAG) & has_after)
            def _():
                pl.semaphore_wait(kv_ready, 1)

            project(i - 4 * LAG)

            @pl.when(i >= 4 * LAG + 3)
            def _():
                relay(i - 4 * LAG - 3)
        return 0

    lax.fori_loop(0, CX + 4 * LAG, gather, 0)

    for chunk in range(CX - 3, CX):
        relay(chunk)

    for n in range(5, z_end):
        out_copy(n, 0).wait_recv()
        out_copy(n + n_zed - 1, 1).start()

    def kv_wait(chunk, _):
        kv_landed(kv_received, chunk)
        return 0

    lax.fori_loop(0, CX, kv_wait, 0)

    def widen(n, _):
        rows = pl.ds(pl.multiple_of(n * SEG, SEG), SEG)
        wide[0, rows, :] = kv[n][:, :DH].astype(F32)
        wide[1, rows, :] = kv[n][:, DH:].astype(F32)
        return 0

    lax.fori_loop(0, 5, widen, 0)
    taps_in.wait()
    taps = cw[:, :, columns].astype(F32)
    for u in range(2):
        for k in range(2):
            mixed = taps[0, k][None, :] * wide[k, pl.ds(1024 * u, SEG, 3), :]
            for r in (1, 2):
                mixed += taps[r, k][None, :] * wide[k, pl.ds(1024 * u + r, SEG, 3), :]
            comp[u, k] = mixed.astype(BF16)

    def attend(u, chunk):
        start = pl.multiple_of(chunk * RC, RC)
        rows = pl.ds(start, RC)
        q = qb[u, rows, :]
        gap = jnp.float32(-1e30)
        no_comp = jnp.where(block >= 1, jnp.float32(0), gap)
        no_mem = jnp.where(block * 4 + core + 2 * u >= 1, jnp.float32(0), gap)
        s_comp = lax.dot_general(q, comp[u, 0], NT, preferred_element_type=F32) + no_comp
        s_mem = lax.dot_general(q, kv[3 + 2 * u, :, :DH], NT, preferred_element_type=F32) + no_mem
        s_own = lax.dot_general(q, kv[4 + 2 * u, :, :DH], NT, preferred_element_type=F32)
        q_pos = start + lax.broadcasted_iota(jnp.int32, (RC, SEG), 0)
        k_pos = lax.broadcasted_iota(jnp.int32, (RC, SEG), 1)
        s_own = jnp.where(k_pos <= q_pos, s_own, gap)
        top = jnp.max(jnp.maximum(jnp.maximum(s_comp, s_mem), s_own), axis=-1, keepdims=True)
        e_comp = jnp.exp2((s_comp - top) * SCALE)
        e_mem = jnp.exp2((s_mem - top) * SCALE)
        e_own = jnp.exp2((s_own - top) * SCALE)
        norm = jnp.sum(e_comp + e_mem + e_own, axis=-1, keepdims=True)
        mixed = dot(e_comp.astype(BF16), comp[u, 1])
        mixed += dot(e_mem.astype(BF16), kv[3 + 2 * u, :, DH:])
        mixed += dot(e_own.astype(BF16), kv[4 + 2 * u, :, DH:])
        cb[y, u, rows, :] = (mixed / norm).astype(BF16)

    def share(i, _):
        @pl.when(i < CC)
        def _():
            for u in range(2):
                attend(u, i)
            for way in (0, 1):
                c_copy(way, 1, i, 1).start()

        forward(c_copy, i, CC, LAGC)

        @pl.when(i >= 4 * LAGC)
        def _():
            landed(c_copy, i, CC, LAGC)

            @pl.when(i == 4 * LAGC)
            def _():
                for n in range(z_end, out_steps):
                    out_copy(n, 0).wait_recv()

            rows = pl.ds(pl.multiple_of((i - 4 * LAGC) * RC, RC), RC)
            whole = jnp.concatenate([cb[slot, hi, rows, :] for slot in (0, 4, 1, 5, 2, 6, 3, 7)], axis=1)
            o_ref[rows, :] = dot(whole, wo[...]).astype(BF16)
        return 0

    lax.fori_loop(0, CC + 4 * LAGC, share, 0)

    def sent(chunk, _):
        for way in (0, 1):
            for dist in (1, 2, 3, 4):
                x_copy(way, dist, chunk, 1).wait_send()
        for copy, needed in zip(kv_copies(chunk), kv_sent):
            when(needed, copy.wait_send)
        return 0

    lax.fori_loop(0, CX, sent, 0)

    def c_sent(chunk, _):
        for way in (0, 1):
            for dist in (1, 2, 3, 4):
                c_copy(way, dist, chunk, 1).wait_send()
        return 0

    lax.fori_loop(0, CC, c_sent, 0)
    for n in range(out_steps):
        out_copy(n, 1).wait_send()


def local(layer_input, w_qkv, comp_weight, w_out, n_seg):
    w = jnp.transpose(w_qkv, (1, 0, 2))
    any_spec = pl.BlockSpec(memory_space=pl.ANY)
    out = pl.pallas_call(
        functools.partial(kernel, n_seg),
        out_shape=jax.ShapeDtypeStruct((SEG, FEAT), BF16),
        in_specs=[any_spec] * 4,
        out_specs=pl.BlockSpec(memory_space=pltpu.VMEM),
        scratch_shapes=[
            pltpu.VMEM((RING, SEG, FEAT), BF16),
            pltpu.VMEM((4 * FEAT, 3 * DH), BF16),
            pltpu.VMEM((3, 2, 2 * DH), BF16),
            pltpu.VMEM((2, 8, FEAT), BF16),
            pltpu.VMEM((RING * DH, FEAT), BF16),
            pltpu.VMEM((7, SEG, 2 * DH), BF16),
            pltpu.VMEM((2, 5 * SEG + 8, DH), F32),
            pltpu.VMEM((2, 2, SEG, DH), BF16),
            pltpu.VMEM((2 * RX, 4 * FEAT), BF16),
            pltpu.VMEM((2, SEG, DH), BF16),
            pltpu.VMEM((RING, 2, SEG, DH), BF16),
            pltpu.SemaphoreType.DMA((6,)),
            pltpu.SemaphoreType.DMA((2, 4, CX)),
            pltpu.SemaphoreType.DMA((2, 4, CX)),
            pltpu.SemaphoreType.DMA((6, CX)),
            pltpu.SemaphoreType.DMA((7, CX)),
            pltpu.SemaphoreType.DMA((2, 4, CC)),
            pltpu.SemaphoreType.DMA((2, 4, CC)),
            pltpu.SemaphoreType.DMA((3 + n_seg // 8,)),
            pltpu.SemaphoreType.DMA((3 + n_seg // 8,)),
            pltpu.SemaphoreType.REGULAR,
            pltpu.SemaphoreType.REGULAR,
            pltpu.SemaphoreType.REGULAR,
            pltpu.SemaphoreType.REGULAR,
        ],
        compiler_params=pltpu.CompilerParams(
            collective_id=0, has_side_effects=True, vmem_limit_bytes=60 << 20
        ),
        cost_estimate=pl.CostEstimate(
            flops=3 * 10**9, bytes_accessed=200 * 10**6, transcendentals=2 * 10**6
        ),
        name="ring_layer",
    )(layer_input[0], w, comp_weight, w_out)
    return out[None]


def solution(mesh):
    return jax.shard_map(
        functools.partial(local, n_seg=mesh.shape["seg"]),
        mesh=mesh,
        in_specs=(
            P(None, "seg", "head"),
            P(None, None, "head"),
            P(None, None, "head"),
            P("seg", "head"),
        ),
        out_specs=P(None, "seg", "head"),
        check_vma=False,
    )
```

```python
import functools
import math

import jax
import jax.numpy as jnp
from jax import lax
from jax.experimental import pallas as pl
from jax.experimental.pallas import tpu as pltpu
from jax.sharding import PartitionSpec as P

MESH = pl.DeviceIdType.MESH
F32, BF16 = jnp.float32, jnp.bfloat16
DH = 128
RING = 8
SEG = 512
FEAT = 512
CX = 8
RX = SEG // CX
CC = 4
LAG = 2
LAGC = 3
WZ = 6
RC = SEG // CC
SCALE = math.log2(math.e) / math.sqrt(DH)
NT = (((1,), (1,)), ((), ()))


def when(needed, act):
    if needed is True:
        act()
    else:
        pl.when(needed)(act)


def dot(a, b):
    return jnp.dot(a, b, preferred_element_type=F32)


def kernel(n_seg, x_hbm, w_hbm, cw_hbm, wo_hbm, o_ref, xb, wb, cw, w8, wo, kv, wide, comp, nb, qb,
           cb, lsem, xs, xr, ks, kr, cs, cr, ws, wr, kv_ready, z_ready, x_ready, y_ready):
    seg, lo = lax.axis_index("seg"), lax.axis_index("head")
    core, hi, block = seg % 2, (seg // 2) % 2, seg // 4
    y = hi * 4 + lo
    n_block = n_seg // 4

    def on_ring(pos):
        return (block * 4 + (pos // 4) * 2 + core, pos % 4)

    up, down = on_ring((y + 1) % RING), on_ring((y + RING - 1) % RING)
    sibling = (block * 4 + hi * 2 + 1 - core, lo)
    after = (((block + 1) % n_block) * 4 + hi * 2 + core, lo)
    before = (((block + n_block - 1) % n_block) * 4 + hi * 2 + core, lo)

    zed, ex = block // 4, block % 4
    n_zed = n_block // 4
    across = (block * 4 + (1 - hi) * 2 + core, lo)
    rows_x = [((zed * 4 + (ex + d) % 4) * 4 + hi * 2 + core, lo) for d in range(1, 4)]
    rows_z = [((((zed + d) % n_zed) * 4 + ex) * 4 + hi * 2 + core, lo) for d in range(1, n_zed)]

    own = pltpu.make_async_copy(x_hbm, xb.at[y], lsem.at[0])
    own.start()
    own_out = pltpu.make_async_copy(wo_hbm, w8.at[core], lsem.at[4])
    own_out.start()
    taps_in = pltpu.make_async_copy(cw_hbm, cw, lsem.at[5])
    taps_in.start()
    columns = pl.ds(pl.multiple_of(hi * DH, DH), DH)
    loads = []
    for i in range(3):
        load = pltpu.make_async_copy(
            w_hbm.at[i, :, columns], wb.at[:, pl.ds(i * DH, DH)], lsem.at[1 + i]
        )
        load.start()
        loads.append(load)

    has_before, has_after = block > 0, block < n_block - 1

    @pl.when(block == 0)
    def _():
        kv[0:4] = jnp.zeros((4, SEG, 2 * DH), BF16)

    barrier = pltpu.get_barrier_semaphore()

    def signal(sem, device):
        pl.semaphore_signal(sem, inc=1, device_id=device, device_id_type=MESH)

    near = (up, down, sibling)
    for device in near:
        signal(barrier, device)

    pl.when(has_after)(functools.partial(signal, barrier, after))
    pl.when(hi == 0)(functools.partial(signal, barrier, across))
    for d, device in enumerate(rows_x, 1):
        pl.when(ex + d < 4)(functools.partial(signal, barrier, device))
    for d, device in enumerate(rows_z, 1):
        pl.when(zed + d < n_zed)(functools.partial(signal, barrier, device))
    pl.semaphore_wait(barrier, len(near) + zed + ex + hi + jnp.where(has_before, 1, 0))

    pl.when(has_before)(functools.partial(signal, kv_ready, before))
    pl.when(hi == 1)(functools.partial(signal, y_ready, across))
    for d, device in enumerate(rows_x, 1):
        pl.when(ex + d >= 4)(functools.partial(signal, x_ready, device))
    for d, device in enumerate(rows_z, 1):
        pl.when(zed + d >= n_zed)(functools.partial(signal, z_ready, device))

    def out_copy(n, hop):
        back = 1 - hop
        if n == 0:
            at, device = w8.at[core if hop else 1 - core], sibling
        elif n == 1:
            start = (block * 2 + (hi if hop else 1 - hi)) * 16
            at, device = wo.at[pl.ds(pl.multiple_of(start, 16), 16)], across
        elif n < 5:
            d = n - 1
            start = (zed * 4 + (ex + 4 - d * back) % 4) * 32
            at, device = wo.at[pl.ds(pl.multiple_of(start, 32), 32)], rows_x[d - 1]
        else:
            d = (n - 5) % (n_zed - 1) + 1
            if n < 4 + n_zed:
                start = ((zed + n_zed - d * back) % n_zed) * 128 + core * 64
                device = rows_z[d - 1]
            else:
                start = ((zed + n_zed - d) % n_zed) * 128 + (core if hop else 1 - core) * 64
                device = sibling
            at = wo.at[pl.ds(pl.multiple_of(start, 64), 64)]
        return pltpu.make_async_remote_copy(
            src_ref=at, dst_ref=at, send_sem=ws.at[n], recv_sem=wr.at[n],
            device_id=device, device_id_type=MESH,
        )

    out_steps, z_end = 3 + 2 * n_zed, 4 + n_zed

    def gather_out(i):
        @pl.when(i == 0)
        def _():
            own_out.wait()
            out_copy(0, 1).start()

        @pl.when(i == 2)
        def _():
            out_copy(0, 0).wait_recv()
            pair = jnp.concatenate([w8[0].astype(F32), w8[1].astype(F32)], axis=0)
            wo[pl.ds(pl.multiple_of((block * 2 + hi) * 16, 16), 16), :] = pair.astype(BF16)

            @pl.when(hi == 0)
            def _():
                pl.semaphore_wait(y_ready, 1)

            out_copy(1, 1).start()

        @pl.when(i == 4)
        def _():
            out_copy(1, 0).wait_recv()

            @pl.when(ex < 3)
            def _():
                pl.semaphore_wait(x_ready, 3 - ex)

            for n in range(2, 5):
                out_copy(n, 1).start()

        @pl.when(i == WZ)
        def _():
            for n in range(2, 5):
                out_copy(n, 0).wait_recv()

            @pl.when(zed < n_zed - 1)
            def _():
                pl.semaphore_wait(z_ready, n_zed - 1 - zed)

            for n in range(5, z_end):
                out_copy(n, 1).start()


    def ring_copy(view, ssem, rsem, way, dist, chunk, hop):
        step = dist - hop
        slot = (y + RING - step) % RING if way == 0 else (y + step) % RING
        ref = view(slot, way, dist, chunk)
        return pltpu.make_async_remote_copy(
            src_ref=ref,
            dst_ref=ref,
            send_sem=ssem.at[way, dist - 1, chunk],
            recv_sem=rsem.at[way, dist - 1, chunk],
            device_id=up if way == 0 else down,
            device_id_type=MESH,
        )

    def x_view(slot, way, dist, chunk):
        if dist < 4:
            return xb.at[slot, pl.ds(pl.multiple_of(chunk * RX, RX), RX)]
        half = RX // 2
        return xb.at[slot, pl.ds(pl.multiple_of(chunk * RX + way * half, half), half)]

    def c_copies(way, dist, chunk, hop):
        step = dist - hop
        slot = (y + RING - step) % RING if way == 0 else (y + step) % RING
        place = slot % 4 if way == 0 else 3 - slot % 4
        theirs, size = 1 - slot // 4, RC
        start = pl.multiple_of(chunk * RC, RC)

        def copy(ref):
            return pltpu.make_async_remote_copy(
                src_ref=ref, dst_ref=ref, send_sem=cs.at[way, dist - 1, chunk],
                recv_sem=cr.at[way, dist - 1, chunk],
                device_id=up if way == 0 else down, device_id_type=MESH,
            )

        if dist == 4:
            half = pl.ds(pl.multiple_of(start + way * (size // 2), size // 2), size // 2)
            return (
                (place == 3, copy(cb.at[slot, theirs, pl.ds(start, size)])),
                ((place == 1) | (place == 2), copy(cb.at[slot, theirs, half])),
            )
        crossing = place + dist >= 4
        unit = jnp.where(crossing, theirs, 1 - theirs)
        single = crossing | (place == 0)
        return (
            (single, copy(cb.at[slot, unit, pl.ds(start, size)])),
            (jnp.logical_not(single), copy(cb.at[slot, :, pl.ds(start, size)])),
        )

    def c_start(way, dist, chunk):
        for needed, copy in c_copies(way, dist, chunk, 1):
            pl.when(needed)(copy.start)

    def c_recv(way, dist, chunk):
        for needed, copy in c_copies(way, dist, chunk, 0):
            pl.when(needed)(copy.wait_recv)

    def c_send_done(way, dist, chunk):
        for needed, copy in c_copies(way, dist, chunk, 1):
            pl.when(needed)(copy.wait_send)

    x_copy = functools.partial(ring_copy, x_view, xs, xr)

    def x_start(way, dist, chunk):
        x_copy(way, dist, chunk, 1).start()

    def x_recv(way, dist, chunk):
        x_copy(way, dist, chunk, 0).wait_recv()

    def forward(recv, start, i, count, lag=LAG):
        for dist in (1, 2, 3):
            @pl.when((i >= dist * lag) & (i < count + dist * lag))
            def _(dist=dist):
                for way in (0, 1):
                    recv(way, dist, i - dist * lag)
                    start(way, dist + 1, i - dist * lag)

    def landed(recv, i, count, lag=LAG):
        for way in (0, 1):
            recv(way, 4, i - 4 * lag)

    def kv_copies(chunk):
        rows = pl.ds(pl.multiple_of(chunk * RX, RX), RX)
        first_core = core == 0
        plan = (
            (4, jnp.where(first_core, 3, 5), sibling),
            (6, 5, sibling),
            (4, 0, after),
            (6, 2, after),
            (jnp.where(first_core, 2, 0), 1, sibling),
            (2, 3, sibling),
        )
        return [
            pltpu.make_async_remote_copy(
                src_ref=kv.at[src, rows],
                dst_ref=kv.at[dst, rows],
                send_sem=ks.at[n, chunk],
                recv_sem=kr.at[dst, chunk],
                device_id=device,
                device_id_type=MESH,
            )
            for n, (src, dst, device) in enumerate(plan)
        ]

    kv_sent = (True, core == 0, has_after, has_after, has_before, (core == 1) & has_before)
    kv_received = ((1, has_before), (3, (core == 1) | has_before), (5, True))

    def kv_landed(slots, chunk):
        rows = pl.ds(pl.multiple_of(chunk * RX, RX), RX)
        for dst, needed in slots:
            copy = pltpu.make_async_remote_copy(
                src_ref=kv.at[dst, rows], dst_ref=kv.at[dst, rows], send_sem=ks.at[0, chunk],
                recv_sem=kr.at[dst, chunk], device_id=sibling, device_id_type=MESH,
            )
            when(needed, copy.wait_recv)

    def relay(chunk):
        kv_landed(((0, has_before), (2, has_before)), chunk)
        for copy, needed in zip(kv_copies(chunk)[4:], kv_sent[4:]):
            when(needed, copy.start)

    def project(chunk):
        rows = pl.ds(pl.multiple_of(chunk * RX, RX), RX)
        for u in range(2):
            parts = [xb[4 * u + f, rows, :].astype(F32) for f in range(4)]
            total = parts[0] + parts[1] + parts[2] + parts[3]
            mean = jnp.sum(total, axis=-1, keepdims=True) / (4 * FEAT)
            parts = [p - mean for p in parts]
            square = sum(p * p for p in parts[1:]) + parts[0] * parts[0]
            var = jnp.sum(square, axis=-1, keepdims=True) / (4 * FEAT)
            rstd = lax.rsqrt(var + 1e-05)
            for f in range(4):
                nb[u * RX:(u + 1) * RX, f * FEAT:(f + 1) * FEAT] = (parts[f] * rstd).astype(BF16)
        out = dot(nb[...], wb[...]).astype(BF16)
        for u in range(2):
            part = out[u * RX:(u + 1) * RX]
            qb[u, rows, :] = part[:, :DH]
            kv[4 + 2 * u, rows, :] = part[:, DH:]
        for copy, needed in zip(kv_copies(chunk)[:4], kv_sent[:4]):
            when(needed, copy.start)

    own.wait()

    def gather(i, _):
        @pl.when(i < CX)
        def _():
            for way in (0, 1):
                x_copy(way, 1, i, 1).start()

        forward(x_recv, x_start, i, CX)
        gather_out(i)

        @pl.when(i == 3)
        def _():
            for load in loads:
                load.wait()

        @pl.when(i >= 4 * LAG)
        def _():
            landed(x_recv, i, CX)

            @pl.when((i == 4 * LAG) & has_after)
            def _():
                pl.semaphore_wait(kv_ready, 1)

            project(i - 4 * LAG)

            @pl.when(i >= 4 * LAG + 3)
            def _():
                relay(i - 4 * LAG - 3)
        return 0

    lax.fori_loop(0, CX + 4 * LAG, gather, 0)

    for chunk in range(CX - 3, CX):
        relay(chunk)

    for n in range(5, z_end):
        out_copy(n, 0).wait_recv()
        out_copy(n + n_zed - 1, 1).start()

    def kv_wait(chunk, _):
        kv_landed(kv_received, chunk)
        return 0

    lax.fori_loop(0, CX, kv_wait, 0)

    def widen(n, _):
        rows = pl.ds(pl.multiple_of(n * SEG, SEG), SEG)
        wide[0, rows, :] = kv[n][:, :DH].astype(F32)
        wide[1, rows, :] = kv[n][:, DH:].astype(F32)
        return 0

    lax.fori_loop(0, 5, widen, 0)
    taps_in.wait()
    taps = cw[:, :, columns].astype(F32)
    for u in range(2):
        for k in range(2):
            mixed = taps[0, k][None, :] * wide[k, pl.ds(1024 * u, SEG, 3), :]
            for r in (1, 2):
                mixed += taps[r, k][None, :] * wide[k, pl.ds(1024 * u + r, SEG, 3), :]
            comp[u, k] = mixed.astype(BF16)

    def attend(u, chunk):
        start = pl.multiple_of(chunk * RC, RC)
        rows = pl.ds(start, RC)
        q = qb[u, rows, :]
        gap = jnp.float32(-1e30)
        no_comp = jnp.where(block >= 1, jnp.float32(0), gap)
        no_mem = jnp.where(block * 4 + core + 2 * u >= 1, jnp.float32(0), gap)
        s_comp = lax.dot_general(q, comp[u, 0], NT, preferred_element_type=F32) + no_comp
        s_mem = lax.dot_general(q, kv[3 + 2 * u, :, :DH], NT, preferred_element_type=F32) + no_mem
        s_own = lax.dot_general(q, kv[4 + 2 * u, :, :DH], NT, preferred_element_type=F32)
        q_pos = start + lax.broadcasted_iota(jnp.int32, (RC, SEG), 0)
        k_pos = lax.broadcasted_iota(jnp.int32, (RC, SEG), 1)
        s_own = jnp.where(k_pos <= q_pos, s_own, gap)
        top = jnp.max(jnp.maximum(jnp.maximum(s_comp, s_mem), s_own), axis=-1, keepdims=True)
        e_comp = jnp.exp2((s_comp - top) * SCALE)
        e_mem = jnp.exp2((s_mem - top) * SCALE)
        e_own = jnp.exp2((s_own - top) * SCALE)
        norm = jnp.sum(e_comp + e_mem + e_own, axis=-1, keepdims=True)
        mixed = dot(e_comp.astype(BF16), comp[u, 1])
        mixed += dot(e_mem.astype(BF16), kv[3 + 2 * u, :, DH:])
        mixed += dot(e_own.astype(BF16), kv[4 + 2 * u, :, DH:])
        cb[y, u, rows, :] = (mixed / norm).astype(BF16)

    def share(i, _):
        @pl.when(i < CC)
        def _():
            for u in range(2):
                attend(u, i)
            for way in (0, 1):
                c_start(way, 1, i)

        forward(c_recv, c_start, i, CC, LAGC)

        @pl.when(i >= 4 * LAGC)
        def _():
            landed(c_recv, i, CC, LAGC)

            @pl.when(i == 4 * LAGC)
            def _():
                for n in range(z_end, out_steps):
                    out_copy(n, 0).wait_recv()

            rows = pl.ds(pl.multiple_of((i - 4 * LAGC) * RC, RC), RC)
            whole = jnp.concatenate([cb[slot, hi, rows, :] for slot in (0, 4, 1, 5, 2, 6, 3, 7)], axis=1)
            o_ref[rows, :] = dot(whole, wo[...]).astype(BF16)
        return 0

    lax.fori_loop(0, CC + 4 * LAGC, share, 0)

    def sent(chunk, _):
        for way in (0, 1):
            for dist in (1, 2, 3, 4):
                x_copy(way, dist, chunk, 1).wait_send()
        for copy, needed in zip(kv_copies(chunk), kv_sent):
            when(needed, copy.wait_send)
        return 0

    lax.fori_loop(0, CX, sent, 0)

    def c_sent(chunk, _):
        for way in (0, 1):
            for dist in (1, 2, 3, 4):
                c_send_done(way, dist, chunk)
        return 0

    lax.fori_loop(0, CC, c_sent, 0)
    for n in range(out_steps):
        out_copy(n, 1).wait_send()


def local(layer_input, w_qkv, comp_weight, w_out, n_seg):
    w = jnp.transpose(w_qkv, (1, 0, 2))
    any_spec = pl.BlockSpec(memory_space=pl.ANY)
    out = pl.pallas_call(
        functools.partial(kernel, n_seg),
        out_shape=jax.ShapeDtypeStruct((SEG, FEAT), BF16),
        in_specs=[any_spec] * 4,
        out_specs=pl.BlockSpec(memory_space=pltpu.VMEM),
        scratch_shapes=[
            pltpu.VMEM((RING, SEG, FEAT), BF16),
            pltpu.VMEM((4 * FEAT, 3 * DH), BF16),
            pltpu.VMEM((3, 2, 2 * DH), BF16),
            pltpu.VMEM((2, 8, FEAT), BF16),
            pltpu.VMEM((RING * DH, FEAT), BF16),
            pltpu.VMEM((7, SEG, 2 * DH), BF16),
            pltpu.VMEM((2, 5 * SEG + 8, DH), F32),
            pltpu.VMEM((2, 2, SEG, DH), BF16),
            pltpu.VMEM((2 * RX, 4 * FEAT), BF16),
            pltpu.VMEM((2, SEG, DH), BF16),
            pltpu.VMEM((RING, 2, SEG, DH), BF16),
            pltpu.SemaphoreType.DMA((6,)),
            pltpu.SemaphoreType.DMA((2, 4, CX)),
            pltpu.SemaphoreType.DMA((2, 4, CX)),
            pltpu.SemaphoreType.DMA((6, CX)),
            pltpu.SemaphoreType.DMA((7, CX)),
            pltpu.SemaphoreType.DMA((2, 4, CC)),
            pltpu.SemaphoreType.DMA((2, 4, CC)),
            pltpu.SemaphoreType.DMA((3 + n_seg // 8,)),
            pltpu.SemaphoreType.DMA((3 + n_seg // 8,)),
            pltpu.SemaphoreType.REGULAR,
            pltpu.SemaphoreType.REGULAR,
            pltpu.SemaphoreType.REGULAR,
            pltpu.SemaphoreType.REGULAR,
        ],
        compiler_params=pltpu.CompilerParams(
            collective_id=0, has_side_effects=True, vmem_limit_bytes=60 << 20
        ),
        cost_estimate=pl.CostEstimate(
            flops=3 * 10**9, bytes_accessed=200 * 10**6, transcendentals=2 * 10**6
        ),
        name="ring_layer",
    )(layer_input[0], w, comp_weight, w_out)
    return out[None]


def solution(mesh):
    return jax.shard_map(
        functools.partial(local, n_seg=mesh.shape["seg"]),
        mesh=mesh,
        in_specs=(
            P(None, "seg", "head"),
            P(None, None, "head"),
            P(None, None, "head"),
            P("seg", "head"),
        ),
        out_specs=P(None, "seg", "head"),
        check_vma=False,
    )
```

```python
import functools
import math

import jax
import jax.numpy as jnp
from jax import lax
from jax.experimental import pallas as pl
from jax.experimental.pallas import tpu as pltpu
from jax.sharding import PartitionSpec as P

MESH = pl.DeviceIdType.MESH
F32, BF16 = jnp.float32, jnp.bfloat16
DH = 128
RING = 8
SEG = 512
FEAT = 512
CX = 8
RX = SEG // CX
CC = 4
LAG = 2
LAGC = 4
WZ = 6
RC = SEG // CC
SCALE = math.log2(math.e) / math.sqrt(DH)
NT = (((1,), (1,)), ((), ()))


def when(needed, act):
    if needed is True:
        act()
    else:
        pl.when(needed)(act)


def dot(a, b):
    return jnp.dot(a, b, preferred_element_type=F32)


def kernel(n_seg, x_hbm, w_hbm, cw_hbm, wo_hbm, o_ref, xb, wb, cw, w8, wo, kv, wide, comp, nb, qb,
           cb, lsem, xs, xr, ks, kr, cs, cr, ws, wr, kv_ready, z_ready, x_ready, y_ready):
    seg, lo = lax.axis_index("seg"), lax.axis_index("head")
    core, hi, block = seg % 2, (seg // 2) % 2, seg // 4
    y = hi * 4 + lo
    n_block = n_seg // 4

    def on_ring(pos):
        return (block * 4 + (pos // 4) * 2 + core, pos % 4)

    up, down = on_ring((y + 1) % RING), on_ring((y + RING - 1) % RING)
    sibling = (block * 4 + hi * 2 + 1 - core, lo)
    after = (((block + 1) % n_block) * 4 + hi * 2 + core, lo)
    before = (((block + n_block - 1) % n_block) * 4 + hi * 2 + core, lo)

    zed, ex = block // 4, block % 4
    n_zed = n_block // 4
    across = (block * 4 + (1 - hi) * 2 + core, lo)
    rows_x = [((zed * 4 + (ex + d) % 4) * 4 + hi * 2 + core, lo) for d in range(1, 4)]
    rows_z = [((((zed + d) % n_zed) * 4 + ex) * 4 + hi * 2 + core, lo) for d in range(1, n_zed)]

    own = pltpu.make_async_copy(x_hbm, xb.at[y], lsem.at[0])
    own.start()
    own_out = pltpu.make_async_copy(wo_hbm, w8.at[core], lsem.at[4])
    own_out.start()
    taps_in = pltpu.make_async_copy(cw_hbm, cw, lsem.at[5])
    taps_in.start()
    columns = pl.ds(pl.multiple_of(hi * DH, DH), DH)
    loads = []
    for i in range(3):
        load = pltpu.make_async_copy(
            w_hbm.at[i, :, columns], wb.at[:, pl.ds(i * DH, DH)], lsem.at[1 + i]
        )
        load.start()
        loads.append(load)

    has_before, has_after = block > 0, block < n_block - 1

    @pl.when(block == 0)
    def _():
        kv[0:4] = jnp.zeros((4, SEG, 2 * DH), BF16)

    barrier = pltpu.get_barrier_semaphore()

    def signal(sem, device):
        pl.semaphore_signal(sem, inc=1, device_id=device, device_id_type=MESH)

    near = (up, down, sibling)
    for device in near:
        signal(barrier, device)

    pl.when(has_after)(functools.partial(signal, barrier, after))
    pl.when(hi == 0)(functools.partial(signal, barrier, across))
    for d, device in enumerate(rows_x, 1):
        pl.when(ex + d < 4)(functools.partial(signal, barrier, device))
    for d, device in enumerate(rows_z, 1):
        pl.when(zed + d < n_zed)(functools.partial(signal, barrier, device))
    pl.semaphore_wait(barrier, len(near) + zed + ex + hi + jnp.where(has_before, 1, 0))

    pl.when(has_before)(functools.partial(signal, kv_ready, before))
    pl.when(hi == 1)(functools.partial(signal, y_ready, across))
    for d, device in enumerate(rows_x, 1):
        pl.when(ex + d >= 4)(functools.partial(signal, x_ready, device))
    for d, device in enumerate(rows_z, 1):
        pl.when(zed + d >= n_zed)(functools.partial(signal, z_ready, device))

    def out_copy(n, hop):
        back = 1 - hop
        if n == 0:
            at, device = w8.at[core if hop else 1 - core], sibling
        elif n == 1:
            start = (block * 2 + (hi if hop else 1 - hi)) * 16
            at, device = wo.at[pl.ds(pl.multiple_of(start, 16), 16)], across
        elif n < 5:
            d = n - 1
            start = (zed * 4 + (ex + 4 - d * back) % 4) * 32
            at, device = wo.at[pl.ds(pl.multiple_of(start, 32), 32)], rows_x[d - 1]
        else:
            d = (n - 5) % (n_zed - 1) + 1
            if n < 4 + n_zed:
                start = ((zed + n_zed - d * back) % n_zed) * 128 + core * 64
                device = rows_z[d - 1]
            else:
                start = ((zed + n_zed - d) % n_zed) * 128 + (core if hop else 1 - core) * 64
                device = sibling
            at = wo.at[pl.ds(pl.multiple_of(start, 64), 64)]
        return pltpu.make_async_remote_copy(
            src_ref=at, dst_ref=at, send_sem=ws.at[n], recv_sem=wr.at[n],
            device_id=device, device_id_type=MESH,
        )

    out_steps, z_end = 3 + 2 * n_zed, 4 + n_zed

    def gather_out(i):
        @pl.when(i == 0)
        def _():
            own_out.wait()
            out_copy(0, 1).start()

        @pl.when(i == 2)
        def _():
            out_copy(0, 0).wait_recv()
            pair = jnp.concatenate([w8[0].astype(F32), w8[1].astype(F32)], axis=0)
            wo[pl.ds(pl.multiple_of((block * 2 + hi) * 16, 16), 16), :] = pair.astype(BF16)

            @pl.when(hi == 0)
            def _():
                pl.semaphore_wait(y_ready, 1)

            out_copy(1, 1).start()

        @pl.when(i == 4)
        def _():
            out_copy(1, 0).wait_recv()

            @pl.when(ex < 3)
            def _():
                pl.semaphore_wait(x_ready, 3 - ex)

            for n in range(2, 5):
                out_copy(n, 1).start()

        @pl.when(i == WZ)
        def _():
            for n in range(2, 5):
                out_copy(n, 0).wait_recv()

            @pl.when(zed < n_zed - 1)
            def _():
                pl.semaphore_wait(z_ready, n_zed - 1 - zed)

            for n in range(5, z_end):
                out_copy(n, 1).start()


    def ring_copy(view, ssem, rsem, way, dist, chunk, hop):
        step = dist - hop
        slot = (y + RING - step) % RING if way == 0 else (y + step) % RING
        ref = view(slot, way, dist, chunk)
        return pltpu.make_async_remote_copy(
            src_ref=ref,
            dst_ref=ref,
            send_sem=ssem.at[way, dist - 1, chunk],
            recv_sem=rsem.at[way, dist - 1, chunk],
            device_id=up if way == 0 else down,
            device_id_type=MESH,
        )

    def x_view(slot, way, dist, chunk):
        if dist < 4:
            return xb.at[slot, pl.ds(pl.multiple_of(chunk * RX, RX), RX)]
        half = RX // 2
        return xb.at[slot, pl.ds(pl.multiple_of(chunk * RX + way * half, half), half)]

    def c_copies(way, dist, chunk, hop):
        step = dist - hop
        slot = (y + RING - step) % RING if way == 0 else (y + step) % RING
        place = slot % 4 if way == 0 else 3 - slot % 4
        theirs, size = 1 - slot // 4, RC
        start = pl.multiple_of(chunk * RC, RC)

        def copy(ref):
            return pltpu.make_async_remote_copy(
                src_ref=ref, dst_ref=ref, send_sem=cs.at[way, dist - 1, chunk],
                recv_sem=cr.at[way, dist - 1, chunk],
                device_id=up if way == 0 else down, device_id_type=MESH,
            )

        if dist == 4:
            half = pl.ds(pl.multiple_of(start + way * (size // 2), size // 2), size // 2)
            return (
                (place == 3, copy(cb.at[slot, theirs, pl.ds(start, size)])),
                ((place == 1) | (place == 2), copy(cb.at[slot, theirs, half])),
            )
        crossing = place + dist >= 4
        unit = jnp.where(crossing, theirs, 1 - theirs)
        single = crossing | (place == 0)
        return (
            (single, copy(cb.at[slot, unit, pl.ds(start, size)])),
            (jnp.logical_not(single), copy(cb.at[slot, :, pl.ds(start, size)])),
        )

    def c_start(way, dist, chunk):
        for needed, copy in c_copies(way, dist, chunk, 1):
            pl.when(needed)(copy.start)

    def c_recv(way, dist, chunk):
        for needed, copy in c_copies(way, dist, chunk, 0):
            pl.when(needed)(copy.wait_recv)

    def c_send_done(way, dist, chunk):
        for needed, copy in c_copies(way, dist, chunk, 1):
            pl.when(needed)(copy.wait_send)

    x_copy = functools.partial(ring_copy, x_view, xs, xr)

    def x_start(way, dist, chunk):
        x_copy(way, dist, chunk, 1).start()

    def x_recv(way, dist, chunk):
        x_copy(way, dist, chunk, 0).wait_recv()

    def forward(recv, start, i, count, lag=LAG):
        for dist in (1, 2, 3):
            @pl.when((i >= dist * lag) & (i < count + dist * lag))
            def _(dist=dist):
                for way in (0, 1):
                    recv(way, dist, i - dist * lag)
                    start(way, dist + 1, i - dist * lag)

    def landed(recv, i, count, lag=LAG):
        for way in (0, 1):
            recv(way, 4, i - 4 * lag)

    def kv_copies(chunk):
        rows = pl.ds(pl.multiple_of(chunk * RX, RX), RX)
        first_core = core == 0
        plan = (
            (4, jnp.where(first_core, 3, 5), sibling),
            (6, 5, sibling),
            (4, 0, after),
            (6, 2, after),
            (jnp.where(first_core, 2, 0), 1, sibling),
            (2, 3, sibling),
        )
        return [
            pltpu.make_async_remote_copy(
                src_ref=kv.at[src, rows],
                dst_ref=kv.at[dst, rows],
                send_sem=ks.at[n, chunk],
                recv_sem=kr.at[dst, chunk],
                device_id=device,
                device_id_type=MESH,
            )
            for n, (src, dst, device) in enumerate(plan)
        ]

    kv_sent = (True, core == 0, has_after, has_after, has_before, (core == 1) & has_before)
    kv_received = ((1, has_before), (3, (core == 1) | has_before), (5, True))

    def kv_landed(slots, chunk):
        rows = pl.ds(pl.multiple_of(chunk * RX, RX), RX)
        for dst, needed in slots:
            copy = pltpu.make_async_remote_copy(
                src_ref=kv.at[dst, rows], dst_ref=kv.at[dst, rows], send_sem=ks.at[0, chunk],
                recv_sem=kr.at[dst, chunk], device_id=sibling, device_id_type=MESH,
            )
            when(needed, copy.wait_recv)

    def widen(n, rows):
        for k in range(2):
            to = pl.ds(pl.multiple_of(n * SEG + rows.start, RX), RX)
            wide[k, to, :] = kv[n, rows, k * DH:(k + 1) * DH].astype(F32)

    def relay(chunk):
        kv_landed(((0, has_before), (2, has_before)), chunk)
        for copy, needed in zip(kv_copies(chunk)[4:], kv_sent[4:]):
            when(needed, copy.start)
        for n in (0, 2, 4):
            widen(n, pl.ds(pl.multiple_of(chunk * RX, RX), RX))

    def project(chunk):
        rows = pl.ds(pl.multiple_of(chunk * RX, RX), RX)
        for u in range(2):
            parts = [xb[4 * u + f, rows, :].astype(F32) for f in range(4)]
            total = parts[0] + parts[1] + parts[2] + parts[3]
            mean = jnp.sum(total, axis=-1, keepdims=True) / (4 * FEAT)
            parts = [p - mean for p in parts]
            square = sum(p * p for p in parts[1:]) + parts[0] * parts[0]
            var = jnp.sum(square, axis=-1, keepdims=True) / (4 * FEAT)
            rstd = lax.rsqrt(var + 1e-05)
            for f in range(4):
                nb[u * RX:(u + 1) * RX, f * FEAT:(f + 1) * FEAT] = (parts[f] * rstd).astype(BF16)
        out = dot(nb[...], wb[...]).astype(BF16)
        for u in range(2):
            part = out[u * RX:(u + 1) * RX]
            qb[u, rows, :] = part[:, :DH]
            kv[4 + 2 * u, rows, :] = part[:, DH:]
        for copy, needed in zip(kv_copies(chunk)[:4], kv_sent[:4]):
            when(needed, copy.start)

    own.wait()

    def gather(i, _):
        @pl.when(i < CX)
        def _():
            for way in (0, 1):
                x_copy(way, 1, i, 1).start()

        forward(x_recv, x_start, i, CX)
        gather_out(i)

        @pl.when(i == 3)
        def _():
            for load in loads:
                load.wait()

        @pl.when(i >= 4 * LAG)
        def _():
            landed(x_recv, i, CX)

            @pl.when((i == 4 * LAG) & has_after)
            def _():
                pl.semaphore_wait(kv_ready, 1)

            project(i - 4 * LAG)

            @pl.when(i >= 4 * LAG + 3)
            def _():
                relay(i - 4 * LAG - 3)
        return 0

    lax.fori_loop(0, CX + 4 * LAG, gather, 0)

    for chunk in range(CX - 3, CX):
        relay(chunk)

    for n in range(5, z_end):
        out_copy(n, 0).wait_recv()
        out_copy(n + n_zed - 1, 1).start()

    def kv_wait(chunk, _):
        kv_landed(kv_received, chunk)
        return 0

    lax.fori_loop(0, CX, kv_wait, 0)

    def widen_rest(chunk, _):
        for n in (1, 3):
            widen(n, pl.ds(pl.multiple_of(chunk * RX, RX), RX))
        return 0

    lax.fori_loop(0, CX, widen_rest, 0)
    taps_in.wait()
    taps = cw[:, :, columns].astype(F32)
    for u in range(2):
        for k in range(2):
            mixed = taps[0, k][None, :] * wide[k, pl.ds(1024 * u, SEG, 3), :]
            for r in (1, 2):
                mixed += taps[r, k][None, :] * wide[k, pl.ds(1024 * u + r, SEG, 3), :]
            comp[u, k] = mixed.astype(BF16)

    def attend(u, chunk):
        start = pl.multiple_of(chunk * RC, RC)
        rows = pl.ds(start, RC)
        q = qb[u, rows, :]
        gap = jnp.float32(-1e30)
        no_comp = jnp.where(block >= 1, jnp.float32(0), gap)
        no_mem = jnp.where(block * 4 + core + 2 * u >= 1, jnp.float32(0), gap)
        s_comp = lax.dot_general(q, comp[u, 0], NT, preferred_element_type=F32) + no_comp
        s_mem = lax.dot_general(q, kv[3 + 2 * u, :, :DH], NT, preferred_element_type=F32) + no_mem
        s_own = lax.dot_general(q, kv[4 + 2 * u, :, :DH], NT, preferred_element_type=F32)
        q_pos = start + lax.broadcasted_iota(jnp.int32, (RC, SEG), 0)
        k_pos = lax.broadcasted_iota(jnp.int32, (RC, SEG), 1)
        s_own = jnp.where(k_pos <= q_pos, s_own, gap)
        top = jnp.max(jnp.maximum(jnp.maximum(s_comp, s_mem), s_own), axis=-1, keepdims=True)
        e_comp = jnp.exp2((s_comp - top) * SCALE)
        e_mem = jnp.exp2((s_mem - top) * SCALE)
        e_own = jnp.exp2((s_own - top) * SCALE)
        norm = jnp.sum(e_comp + e_mem + e_own, axis=-1, keepdims=True)
        mixed = dot(e_comp.astype(BF16), comp[u, 1])
        mixed += dot(e_mem.astype(BF16), kv[3 + 2 * u, :, DH:])
        mixed += dot(e_own.astype(BF16), kv[4 + 2 * u, :, DH:])
        cb[y, u, rows, :] = (mixed / norm).astype(BF16)

    def share(i, _):
        @pl.when(i < CC)
        def _():
            for u in range(2):
                attend(u, i)
            for way in (0, 1):
                c_start(way, 1, i)

        forward(c_recv, c_start, i, CC, LAGC)

        @pl.when(i >= 4 * LAGC)
        def _():
            landed(c_recv, i, CC, LAGC)

            @pl.when(i == 4 * LAGC)
            def _():
                for n in range(z_end, out_steps):
                    out_copy(n, 0).wait_recv()

            rows = pl.ds(pl.multiple_of((i - 4 * LAGC) * RC, RC), RC)
            whole = jnp.concatenate([cb[slot, hi, rows, :] for slot in (0, 4, 1, 5, 2, 6, 3, 7)], axis=1)
            o_ref[rows, :] = dot(whole, wo[...]).astype(BF16)
        return 0

    lax.fori_loop(0, CC + 4 * LAGC, share, 0)

    def sent(chunk, _):
        for way in (0, 1):
            for dist in (1, 2, 3, 4):
                x_copy(way, dist, chunk, 1).wait_send()
        for copy, needed in zip(kv_copies(chunk), kv_sent):
            when(needed, copy.wait_send)
        return 0

    lax.fori_loop(0, CX, sent, 0)

    def c_sent(chunk, _):
        for way in (0, 1):
            for dist in (1, 2, 3, 4):
                c_send_done(way, dist, chunk)
        return 0

    lax.fori_loop(0, CC, c_sent, 0)
    for n in range(out_steps):
        out_copy(n, 1).wait_send()


def local(layer_input, w_qkv, comp_weight, w_out, n_seg):
    w = jnp.transpose(w_qkv, (1, 0, 2))
    any_spec = pl.BlockSpec(memory_space=pl.ANY)
    out = pl.pallas_call(
        functools.partial(kernel, n_seg),
        out_shape=jax.ShapeDtypeStruct((SEG, FEAT), BF16),
        in_specs=[any_spec] * 4,
        out_specs=pl.BlockSpec(memory_space=pltpu.VMEM),
        scratch_shapes=[
            pltpu.VMEM((RING, SEG, FEAT), BF16),
            pltpu.VMEM((4 * FEAT, 3 * DH), BF16),
            pltpu.VMEM((3, 2, 2 * DH), BF16),
            pltpu.VMEM((2, 8, FEAT), BF16),
            pltpu.VMEM((RING * DH, FEAT), BF16),
            pltpu.VMEM((7, SEG, 2 * DH), BF16),
            pltpu.VMEM((2, 5 * SEG + 8, DH), F32),
            pltpu.VMEM((2, 2, SEG, DH), BF16),
            pltpu.VMEM((2 * RX, 4 * FEAT), BF16),
            pltpu.VMEM((2, SEG, DH), BF16),
            pltpu.VMEM((RING, 2, SEG, DH), BF16),
            pltpu.SemaphoreType.DMA((6,)),
            pltpu.SemaphoreType.DMA((2, 4, CX)),
            pltpu.SemaphoreType.DMA((2, 4, CX)),
            pltpu.SemaphoreType.DMA((6, CX)),
            pltpu.SemaphoreType.DMA((7, CX)),
            pltpu.SemaphoreType.DMA((2, 4, CC)),
            pltpu.SemaphoreType.DMA((2, 4, CC)),
            pltpu.SemaphoreType.DMA((3 + n_seg // 8,)),
            pltpu.SemaphoreType.DMA((3 + n_seg // 8,)),
            pltpu.SemaphoreType.REGULAR,
            pltpu.SemaphoreType.REGULAR,
            pltpu.SemaphoreType.REGULAR,
            pltpu.SemaphoreType.REGULAR,
        ],
        compiler_params=pltpu.CompilerParams(
            collective_id=0, has_side_effects=True, vmem_limit_bytes=60 << 20
        ),
        cost_estimate=pl.CostEstimate(
            flops=3 * 10**9, bytes_accessed=200 * 10**6, transcendentals=2 * 10**6
        ),
        name="ring_layer",
    )(layer_input[0], w, comp_weight, w_out)
    return out[None]


def solution(mesh):
    return jax.shard_map(
        functools.partial(local, n_seg=mesh.shape["seg"]),
        mesh=mesh,
        in_specs=(
            P(None, "seg", "head"),
            P(None, None, "head"),
            P(None, None, "head"),
            P("seg", "head"),
        ),
        out_specs=P(None, "seg", "head"),
        check_vma=False,
    )
```
